256 devices in a mesh: lat: 16 (over x_lo, y, core), lon: 16 (over x_hi, z).
Axes of the slice: x: 4 (x_hi: 2, x_lo: 2; x = x_hi * 2 + x_lo), y: 4, z: 8, core: 2. Of those that a mesh axis runs over, the one named last changes fastest.
Arguments:
- obs_frac: float32 [16, 16, 2, 1024], P('lat', 'lon'), may hold values from 0 to 1
- obs_field: float32 [16, 16, 3, 1024], P('lat', 'lon'), may hold values from -6 to 6
- dipole_frac: float32 [16, 16, 2, 256], P('lat', 'lon'), may hold values from 0 to 1
- dipole_moment: float32 [16, 16, 256], P('lat', 'lon'), may hold values from -6 to 6
- obs_count: int32 [16, 16], P('lat', 'lon'), may hold values from 256 to 1024, as said below
Outputs:
- gram: float32 [16, 16, 13, 256, 256], P('lat', 'lon')
- rhs: float32 [16, 16, 256], P('lat', 'lon')
The draws below stay inside these ranges and needn't reach their ends.
Inputs may be any that keep to these rules, and one draw needn't show every extreme that they name: `obs_count`: tiles of the first and of the last latitude row hold exactly 1024 observations; every other tile holds between 256 and 512.
All inputs are finite; a program needn't handle non-finite values.
Results may differ from the reference program's by a relative error of at most 0.0003.
Values sent between devices are 32-bit elements; how exact they have to be, the bound alone decides.
A program may use at most 128 MiB of HBM per device.

```python
import math
import jax
import jax.numpy as jnp
from jax import lax

BS = 256
OBS = 1024
LAT_TILES = 16
LON_TILES = 16


def draw_obs_count(key, part):
    middle = jax.random.randint(key, (LAT_TILES, LON_TILES), OBS // 4, OBS // 2 + 1)
    lat_rows = jnp.arange(LAT_TILES)[:, None] + jnp.zeros((LAT_TILES, LON_TILES), jnp.int32)
    polar = (lat_rows == 0) | (lat_rows == LAT_TILES - 1)
    return jnp.where(polar, OBS, middle).astype(jnp.int32)


def block_levels(stream_key, dims, shards, low, top_value):
    level = 1.0
    for axis_at, shards_of in shards:
        draws = jax.random.uniform(jax.random.fold_in(jax.random.fold_in(stream_key, 6), axis_at), (shards_of,), jnp.float32, low / len(shards), top_value / len(shards))
        level = level * jnp.repeat(jnp.exp(draws), dims[axis_at] // shards_of).reshape((-1,) + (1,) * (len(dims) - 1 - axis_at))
    return level


def normal_values(stream_key, shape, spread, limit, cuts=(), kind=jnp.bfloat16):
    factor_of = block_levels(stream_key, shape, cuts, -0.22, 0.18) if cuts else 1.0
    array = jax.random.normal(stream_key, shape, jnp.float32) * spread * factor_of
    return jnp.minimum(jnp.maximum(array, -limit), limit).astype(kind)


def setup_inputs(seed: int = 0) -> dict:
    seeds = jax.random.split(jax.random.key(seed), 6)
    return {
        "obs_frac": jnp.clip(1.0 * jax.random.uniform(seeds[0], (LAT_TILES, LON_TILES, 2, OBS), jnp.float32) ** block_levels(seeds[0], (LAT_TILES, LON_TILES, 2, OBS), ((0, 16), (1, 16)), -0.2, 0.2), 0.0, 1.0),
        "obs_field": normal_values(seeds[1], (LAT_TILES, LON_TILES, 3, OBS), 1.0, 6.0, ((0, 16), (1, 16)), jnp.float32),
        "dipole_frac": jnp.clip(1.0 * jax.random.uniform(seeds[2], (LAT_TILES, LON_TILES, 2, BS), jnp.float32) ** block_levels(seeds[2], (LAT_TILES, LON_TILES, 2, BS), ((0, 16), (1, 16)), -0.2, 0.2), 0.0, 1.0),
        "dipole_moment": normal_values(seeds[3], (LAT_TILES, LON_TILES, BS), 1.0, 6.0, ((0, 16), (1, 16)), jnp.float32),
        "obs_count": draw_obs_count(jax.random.fold_in(seeds[5], 71), 0),
    }


CROSS = ((0, 0), (-1, 0), (1, 0), (0, -1), (0, 1))
OFFSETS = ((0, 0), (-1, 0), (1, 0), (0, -1), (0, 1), (-2, 0), (2, 0), (0, -2), (0, 2), (-1, -1), (-1, 1), (1, -1), (1, 1))
OBS_RADIUS = 1.06
SOURCE_RADIUS = 0.99
KERNEL_SCALE = 1e-4
HUBER_EDGE = 0.8
DEGREE = math.pi / 180.0


def place(fraction, lat_index, lon_index, lat_tiles, lon_tiles, radius):
    lat_span = 160.0 * DEGREE / lat_tiles
    latitude = -80.0 * DEGREE + (lat_index + fraction[0]) * lat_span
    longitude = (lon_index + fraction[1]) * (2.0 * math.pi / lon_tiles)
    return radius * jnp.stack([jnp.cos(latitude) * jnp.cos(longitude), jnp.cos(latitude) * jnp.sin(longitude), jnp.sin(latitude)])


def kernel(points, sources):
    separation = points[:, :, None] - sources[:, None, :]
    squared = jnp.sum(separation * separation, axis=0)
    aligned = jnp.sum(sources[:, None, :] * separation, axis=0)
    inverse_cube = squared ** -1.5
    return KERNEL_SCALE * (3.0 * aligned / squared * separation - sources[:, None, :]) * inverse_cube


def moved(tiles_block, lat_step, lon_step):
    tiles_block = jnp.roll(tiles_block, lon_step, axis=1)
    if lat_step == 1:
        tiles_block = jnp.concatenate([jnp.zeros_like(tiles_block[:1]), tiles_block[:-1]], 0)
    elif lat_step == -1:
        tiles_block = jnp.concatenate([tiles_block[1:], jnp.zeros_like(tiles_block[:1])], 0)
    return tiles_block


def reference(obs_frac, obs_field, dipole_frac, dipole_moment, obs_count):
    lat_ids = jnp.arange(LAT_TILES, dtype=jnp.int32)
    lon_ids = jnp.arange(LON_TILES, dtype=jnp.int32)

    def place_row(fractions, lat_index):
        return jax.vmap(lambda member, lon_index: place(member, lat_index, lon_index, LAT_TILES, LON_TILES, SOURCE_RADIUS))(fractions, lon_ids)

    sources_all = jax.vmap(place_row)(dipole_frac, lat_ids)
    zero_row = jnp.zeros_like(sources_all[:1])
    sources_pad = jnp.concatenate([zero_row, sources_all, zero_row], 0)
    zero_moment = jnp.zeros_like(dipole_moment[:1])
    moments_pad = jnp.concatenate([zero_moment, dipole_moment, zero_moment], 0)

    def tile_work(tile_number):
        lat_row = tile_number // LON_TILES
        lon_col = tile_number % LON_TILES
        source_list = []
        moment_list = []
        for lat_step, lon_step in CROSS:
            source_list.append(sources_pad[lat_row + 1 + lat_step, (lon_col + lon_step) % LON_TILES])
            moment_list.append(moments_pad[lat_row + 1 + lat_step, (lon_col + lon_step) % LON_TILES])
        sources = jnp.concatenate(source_list, 1)
        moments = jnp.concatenate(moment_list, 0)
        points = place(obs_frac[lat_row, lon_col], lat_row, lon_col, LAT_TILES, LON_TILES, OBS_RADIUS)
        coupling = kernel(points, sources)
        predicted = jnp.einsum('coj,j->co', coupling, moments, precision=lax.Precision.HIGHEST)
        residual = obs_field[lat_row, lon_col] - predicted
        present = (jnp.arange(OBS, dtype=jnp.int32) < obs_count[lat_row, lon_col]).astype(jnp.float32)
        weight = present * HUBER_EDGE / jnp.maximum(jnp.abs(residual), HUBER_EDGE)
        coupling_low = coupling.astype(jnp.bfloat16)
        weighted_low = (weight[:, :, None] * coupling).astype(jnp.bfloat16)
        partial_value = jnp.einsum('coi,coj->ij', weighted_low.astype(jnp.float32), coupling_low.astype(jnp.float32), precision=lax.Precision.HIGHEST)
        right_side = jnp.einsum('coi,co->i', coupling, weight * residual, precision=lax.Precision.HIGHEST)
        return partial_value, right_side

    partials, rights = lax.map(tile_work, jnp.arange(LAT_TILES * LON_TILES, dtype=jnp.int32))
    pair_blocks = partials.reshape(LAT_TILES, LON_TILES, 5, BS, 5, BS)
    right_blocks = rights.reshape(LAT_TILES, LON_TILES, 5, BS)
    blocks = [jnp.zeros((LAT_TILES, LON_TILES, BS, BS), jnp.float32) for offset in OFFSETS]
    rhs = jnp.zeros((LAT_TILES, LON_TILES, BS), jnp.float32)
    for first, (lat_step, lon_step) in enumerate(CROSS):
        rhs = rhs + moved(right_blocks[:, :, first], lat_step, lon_step)
        for second, (lat_other, lon_other) in enumerate(CROSS):
            target = OFFSETS.index((lat_other - lat_step, lon_other - lon_step))
            blocks[target] = blocks[target] + moved(pair_blocks[:, :, first, :, second, :], lat_step, lon_step)
    gram = jnp.stack(blocks, axis=2)
    return gram, rhs
```

```python
import functools
import math

import jax
import jax.numpy as jnp
import numpy as np
from jax import lax
from jax.experimental import pallas as pl
from jax.experimental.pallas import tpu as pltpu
from jax.sharding import PartitionSpec as P

CROSS = ((0, 0), (-1, 0), (1, 0), (0, -1), (0, 1))
OFFSETS = (
    (0, 0),
    (-1, 0),
    (1, 0),
    (0, -1),
    (0, 1),
    (-2, 0),
    (2, 0),
    (0, -2),
    (0, 2),
    (-1, -1),
    (-1, 1),
    (1, -1),
    (1, 1),
)
OBS_RADIUS = 1.06
SOURCE_RADIUS = 0.99
KERNEL_SCALE = 0.0001
HUBER_EDGE = 0.8
DEGREE = math.pi / 180.0
LAT = 16
LON = 16
BS = 256
OBS = 1024
HALF = 512
SPARE = 13
EDGE = (1.5 * (OBS_RADIUS**2 + SOURCE_RADIUS**2) - 3.0 * SOURCE_RADIUS**2) / 1.5
FOLD = 1.5 * KERNEL_SCALE * EDGE**-1.5
FEATURES = 32
FIELDS = 8


def pass_table():
    table = np.zeros((LAT, 8, FIELDS), np.int32)
    counts = np.zeros((LAT,), np.int32)
    for lat in range(LAT):
        rows = []
        for slot, (lat_step, lon_step) in enumerate(CROSS):
            tile = lat - lat_step
            if not 0 <= tile < LAT:
                continue
            there = [b for b in CROSS if 0 <= tile + b[0] < LAT]
            there.sort(key=lambda b: b != (lat_step, lon_step))
            blocks = [OFFSETS.index((b[0] - lat_step, b[1] - lon_step)) for b in there]
            blocks += [SPARE] * (5 - len(blocks))
            for half in range(2 if tile in (0, LAT - 1) else 1):
                rows.append([slot, half] + blocks + [len(there)])
        counts[lat] = len(rows)
        table[lat, : len(rows)] = rows
    return table, counts


def positions(angles, radius):
    cosine, sine = jnp.cos(angles), jnp.sin(angles)
    ring = radius * cosine[0:1]
    return ring * cosine[1:2], ring * sine[1:2], radius * sine[0:1]


def exchange(count_ref, obs_ref, field_ref, dip_ref, moment_ref, dips, tiles, origin, send_dip, recv_dip, send_obs, recv_obs):
    lat, lon = lax.axis_index("lat"), lax.axis_index("lon")

    def inside(step):
        return (lat + step >= 0) & (lat + step < LAT)

    def device(offset):
        return (lat + offset[0], lax.rem(lon + offset[1] + LON, LON))

    barrier = pltpu.get_barrier_semaphore()
    for offset in OFFSETS[1:]:

        @pl.when(inside(offset[0]))
        def _():
            pl.semaphore_signal(barrier, inc=1, device_id=device(offset), device_id_type=pl.DeviceIdType.MESH)

    def angles(fraction):
        row = lax.broadcasted_iota(jnp.int32, fraction.shape, 0)
        index = jnp.where(row == 0, lat.astype(jnp.float32), lon.astype(jnp.float32))
        span = jnp.where(row == 0, 160.0 * DEGREE / LAT, 2.0 * math.pi / LON)
        base = jnp.where(row == 0, -80.0 * DEGREE, 0.0)
        return base + (index + fraction) * span

    for row, value in enumerate(positions(angles(dip_ref[...]), SOURCE_RADIUS)):
        dips[0, row : row + 1, :] = value
    dips[0, 3:4, :] = moment_ref[...]
    dips[0, 4:8, :] = jnp.zeros((4, BS), jnp.float32)
    dips[SPARE] = jnp.zeros((8, BS), jnp.float32)
    for row, value in enumerate(positions(angles(obs_ref[...]), OBS_RADIUS)):
        tiles[0, row : row + 1, :] = value
    tiles[0, 3:6, :] = field_ref[...]
    slot_index = lax.broadcasted_iota(jnp.int32, (1, OBS), 1)
    tiles[0, 6:7, :] = jnp.where(slot_index < count_ref[0, 0], 1.0, 0.0)
    tiles[0, 7:8, :] = jnp.zeros((1, OBS), jnp.float32)
    origin[...] = jnp.zeros_like(origin)
    for row, value in enumerate(positions(angles(jnp.full((2, 128), 0.5, jnp.float32)), 0.5 * (OBS_RADIUS + SOURCE_RADIUS))):
        origin[row : row + 1, :] = value

    pl.semaphore_wait(barrier, sum(inside(offset[0]).astype(jnp.int32) for offset in OFFSETS[1:]))

    def dip_copy(slot):
        step = OFFSETS[slot]
        return pltpu.make_async_remote_copy(
            src_ref=dips.at[0],
            dst_ref=dips.at[slot],
            send_sem=send_dip.at[slot],
            recv_sem=recv_dip.at[slot],
            device_id=device((-step[0], -step[1])),
            device_id_type=pl.DeviceIdType.MESH,
        )

    def obs_copy(slot):
        return pltpu.make_async_remote_copy(
            src_ref=tiles.at[0],
            dst_ref=tiles.at[slot],
            send_sem=send_obs.at[slot],
            recv_sem=recv_obs.at[slot],
            device_id=device(CROSS[slot]),
            device_id_type=pl.DeviceIdType.MESH,
        )

    for slot in range(1, len(CROSS)):

        @pl.when(inside(CROSS[slot][0]))
        def _():
            obs_copy(slot).start()

    for slot in range(1, len(OFFSETS)):

        @pl.when(inside(-OFFSETS[slot][0]))
        def _():
            dip_copy(slot).start()

    for slot in range(1, len(OFFSETS)):

        @pl.when(inside(OFFSETS[slot][0]))
        def _():
            dip_copy(slot).wait_recv()

        @pl.when(jnp.logical_not(inside(OFFSETS[slot][0])))
        def _():
            dips[slot] = jnp.zeros((8, BS), jnp.float32)

        @pl.when(inside(-OFFSETS[slot][0]))
        def _():
            dip_copy(slot).wait_send()

    for slot in range(1, len(CROSS)):

        @pl.when(inside(-CROSS[slot][0]))
        def _():
            obs_copy(slot).wait_recv()

        @pl.when(jnp.logical_not(inside(-CROSS[slot][0])))
        def _():
            tiles[slot] = jnp.zeros((8, OBS), jnp.float32)

        @pl.when(inside(CROSS[slot][0]))
        def _():
            obs_copy(slot).wait_send()


def thirds(value):
    high = value.astype(jnp.bfloat16).astype(jnp.float32)
    rest = value - high
    middle = rest.astype(jnp.bfloat16).astype(jnp.float32)
    return high, middle, rest - middle


def fill(slabs, parts, squares, flipped):
    high, middle, low = parts
    order = (high, middle, high, low, middle, high) if flipped else (high, high, middle, high, middle, low)
    for row, part in enumerate(order):
        slabs[3 * row : 3 * row + 3, :] = part
    ones = jnp.ones_like(squares[0])
    tail = (ones, ones, ones) + squares if flipped else squares + (ones, ones, ones)
    for row, part in enumerate(tail):
        slabs[18 + row : 19 + row, :] = part
    slabs[24:32, :] = jnp.zeros((8, slabs.shape[1]), jnp.float32)


def couple(squared, points, sources):
    inverse = lax.rsqrt(squared)
    second = inverse * inverse
    third = inverse * second
    fifth = third * second
    along = fifth - third
    across = fifth - third * (1.0 / 3.0)
    return [along * p - across * s for p, s in zip(points, sources)]


def compute(counts, table, dips, tiles, origin, gram, rhs, obs_rows, obs_features, source_features, wide, squared, low, own, weighted, predicted, right, total, slab_s, slab_o, out_sem):
    lat = lax.axis_index("lat")
    passes = counts[lat]
    centre = origin[0:3, 0:1]

    def source_setup(slot, carry):
        raw = dips[slot]
        local = raw[0:3, :] - centre
        scaled = local * (-2.0 / EDGE)
        square = jnp.sum(local * local, axis=0, keepdims=True) * (1.0 / EDGE)
        fill(slab_s, thirds(scaled), thirds(square), True)
        source_features[slot] = slab_s[...].T.astype(jnp.bfloat16)
        columns = raw.T
        for row in range(4):
            column = columns[:, row : row + 1] * (FOLD if row < 3 else 1.0)
            wide[slot, row] = jnp.broadcast_to(column, (BS, 128))
        return carry

    lax.fori_loop(0, 14, source_setup, 0)

    def obs_setup(slot, carry):
        raw = tiles[slot]
        local = raw[0:3, :] - centre
        square = jnp.sum(local * local, axis=0, keepdims=True) * (1.0 / EDGE)
        fill(slab_o, thirds(local), thirds(square), False)
        features = slab_o[...].astype(jnp.bfloat16)
        obs_features[slot, 0] = features[:, :HALF]
        obs_features[slot, 1] = features[:, HALF:]
        scaled = raw[0:3, :] * FOLD
        for half in range(2):
            obs_rows[slot, half, 0:3, :] = scaled[:, half * HALF : (half + 1) * HALF]
            obs_rows[slot, half, 3:7, :] = raw[3:7, half * HALF : (half + 1) * HALF]
        return carry

    lax.fori_loop(0, 5, obs_setup, 0)

    total[...] = jnp.zeros_like(total)
    right[...] = jnp.zeros_like(right)

    def square_block(tile, half, source, to):
        squared[to] = jnp.dot(source_features[source], obs_features[tile, half], preferred_element_type=jnp.float32)

    def couple_block(tile, half, source, position):
        for lane in range(4):
            lanes = slice(lane * 128, lane * 128 + 128)
            points = [obs_rows[tile, half, c : c + 1, lanes] for c in range(3)]
            sums = [jnp.zeros((16, 128), jnp.float32) for c in range(3)]
            for piece in range(16):
                rows = slice(piece * 16, piece * 16 + 16)
                values = couple(squared[position % 3, rows, lanes], points, [wide[source, c, rows] for c in range(3)])
                moment = wide[source, 3, rows]
                for c in range(3):
                    sums[c] = sums[c] + values[c] * moment
                    columns = slice(c * HALF + lane * 128, c * HALF + lane * 128 + 128)
                    low[position, rows, columns] = values[c].astype(jnp.bfloat16)
                    if position == 0:
                        own[rows, columns] = values[c]
            for c in range(3):
                columns = slice(c * HALF + lane * 128, c * HALF + lane * 128 + 128)
                if position == 0:
                    predicted[:, columns] = sums[c]
                else:
                    predicted[:, columns] += sums[c]

    def add_gram(target, position):
        product = lax.dot_general(weighted[...], low[position], (((1,), (1,)), ((), ())), preferred_element_type=jnp.float32)
        total[target] = total[target] + product

    def one_pass(number, before):
        entry = [table[lat, number, field] for field in range(FIELDS)]
        tile, half, sources, blocks = entry[0], entry[1], entry[2:7], entry[7]
        square_block(tile, half, sources[0], 0)
        for position in range(4):
            square_block(tile, half, sources[position + 1], (position + 1) % 3)
            add_gram(before[position], position + 1)
            couple_block(tile, half, sources[position], position)

        @pl.when(blocks == 5)
        def _():
            couple_block(tile, half, sources[4], 4)

        for lane in range(4):
            lanes = slice(lane * 128, lane * 128 + 128)
            present = obs_rows[tile, half, 6:7, lanes] * HUBER_EDGE
            residual, weight = [], []
            for c in range(3):
                columns = slice(c * HALF + lane * 128, c * HALF + lane * 128 + 128)
                value = obs_rows[tile, half, 3 + c : 4 + c, lanes] - jnp.sum(predicted[:, columns], axis=0, keepdims=True)
                residual.append(value)
                weight.append(present / jnp.maximum(jnp.abs(value), HUBER_EDGE))
            for piece in range(16):
                rows = slice(piece * 16, piece * 16 + 16)
                sums = right[rows]
                for c in range(3):
                    columns = slice(c * HALF + lane * 128, c * HALF + lane * 128 + 128)
                    value = own[rows, columns] * weight[c]
                    weighted[rows, columns] = value.astype(jnp.bfloat16)
                    sums = sums + value * residual[c]
                right[rows] = sums
        add_gram(0, 0)
        return tuple(sources[1:])

    last = lax.fori_loop(0, passes, one_pass, (SPARE,) * 4)
    for position in range(4):
        add_gram(last[position], position + 1)
    rhs[...] = jnp.sum(right[...].T, axis=0, keepdims=True)
    copy = pltpu.make_async_copy(total.at[pl.ds(0, 13)], gram, out_sem)
    copy.start()
    copy.wait()


def shards(obs_frac, obs_field, dipole_frac, dipole_moment, obs_count):
    vmem = pl.BlockSpec(memory_space=pltpu.VMEM)
    smem = pl.BlockSpec(memory_space=pltpu.SMEM)
    slots = len(OFFSETS) + 1
    dips, tiles, origin = pl.pallas_call(
        exchange,
        out_shape=(
            jax.ShapeDtypeStruct((slots, 8, BS), jnp.float32),
            jax.ShapeDtypeStruct((5, 8, OBS), jnp.float32),
            jax.ShapeDtypeStruct((8, 128), jnp.float32),
        ),
        in_specs=[smem, vmem, vmem, vmem, vmem],
        out_specs=(vmem, vmem, vmem),
        scratch_shapes=[
            pltpu.SemaphoreType.DMA((len(OFFSETS),)),
            pltpu.SemaphoreType.DMA((len(OFFSETS),)),
            pltpu.SemaphoreType.DMA((len(CROSS),)),
            pltpu.SemaphoreType.DMA((len(CROSS),)),
        ],
        compiler_params=pltpu.CompilerParams(collective_id=0, has_side_effects=True),
        name="exchange",
    )(obs_count, obs_frac[0, 0], obs_field[0, 0], dipole_frac[0, 0], dipole_moment[0])
    gram, rhs = compute_call(dips, tiles, origin)
    return gram[None, None], rhs[None]


def compute_call(dips, tiles, origin, kernel=compute):
    vmem = pl.BlockSpec(memory_space=pltpu.VMEM)
    smem = pl.BlockSpec(memory_space=pltpu.SMEM)
    slots = len(OFFSETS) + 1
    table, counts = pass_table()
    f32, low = jnp.float32, jnp.bfloat16
    return pl.pallas_call(
        kernel,
        out_shape=(jax.ShapeDtypeStruct((13, BS, BS), f32), jax.ShapeDtypeStruct((1, BS), f32)),
        in_specs=[smem, smem, vmem, vmem, vmem],
        out_specs=(pl.BlockSpec(memory_space=pl.ANY), vmem),
        scratch_shapes=[
            pltpu.VMEM((5, 2, 8, HALF), f32),
            pltpu.VMEM((5, 2, FEATURES, HALF), low),
            pltpu.VMEM((slots, BS, FEATURES), low),
            pltpu.VMEM((slots, 4, BS, 128), f32),
            pltpu.VMEM((3, BS, HALF), f32),
            pltpu.VMEM((5, BS, 3 * HALF), low),
            pltpu.VMEM((BS, 3 * HALF), f32),
            pltpu.VMEM((BS, 3 * HALF), low),
            pltpu.VMEM((16, 3 * HALF), f32),
            pltpu.VMEM((BS, 128), f32),
            pltpu.VMEM((slots, BS, BS), f32),
            pltpu.VMEM((FEATURES, BS), f32),
            pltpu.VMEM((FEATURES, OBS), f32),
            pltpu.SemaphoreType.DMA,
        ],
        compiler_params=pltpu.CompilerParams(vmem_limit_bytes=48 * 2**20),
        name="normal_blocks",
    )(jnp.asarray(counts), jnp.asarray(table), dips, tiles, origin)


def solution(mesh):
    in_specs = (
        P("lat", "lon", None, None),
        P("lat", "lon", None, None),
        P("lat", "lon", None, None),
        P("lat", "lon", None),
        P("lat", "lon"),
    )
    out_specs = (P("lat", "lon", None, None, None), P("lat", "lon", None))
    return jax.shard_map(shards, mesh=mesh, in_specs=in_specs, out_specs=out_specs, check_vma=False)
```

```python
import functools
import math

import jax
import jax.numpy as jnp
import numpy as np
from jax import lax
from jax.experimental import pallas as pl
from jax.experimental.pallas import tpu as pltpu
from jax.sharding import PartitionSpec as P

CROSS = ((0, 0), (-1, 0), (1, 0), (0, -1), (0, 1))
OFFSETS = (
    (0, 0),
    (-1, 0),
    (1, 0),
    (0, -1),
    (0, 1),
    (-2, 0),
    (2, 0),
    (0, -2),
    (0, 2),
    (-1, -1),
    (-1, 1),
    (1, -1),
    (1, 1),
)
OBS_RADIUS = 1.06
SOURCE_RADIUS = 0.99
KERNEL_SCALE = 0.0001
HUBER_EDGE = 0.8
DEGREE = math.pi / 180.0
LAT = 16
LON = 16
BS = 256
OBS = 1024
HALF = 512
SPARE = 13
EDGE = (1.5 * (OBS_RADIUS**2 + SOURCE_RADIUS**2) - 3.0 * SOURCE_RADIUS**2) / 1.5
FOLD = 1.5 * KERNEL_SCALE * EDGE**-1.5
FEATURES = 32


def pass_rows(lat):
    rows = []
    for slot, (lat_step, lon_step) in enumerate(CROSS):
        tile = lat - lat_step
        if not 0 <= tile < LAT:
            continue
        there = [b for b in CROSS if 0 <= tile + b[0] < LAT]
        there.sort(key=lambda b: b != (lat_step, lon_step))
        blocks = [OFFSETS.index((b[0] - lat_step, b[1] - lon_step)) for b in there]
        blocks += [SPARE] * (5 - len(blocks))
        for half in range(2 if tile in (0, LAT - 1) else 1):
            rows.append((slot, half, blocks, len(there)))
    return rows


def pass_codes(lat):
    rows = pass_rows(lat)
    codes, ready = [], set(rows[0][2])
    for number, (slot, half, blocks, present) in enumerate(rows):
        after = rows[number + 1][2] if number + 1 < len(rows) else []
        fresh = [block for block in after if block not in ready]
        ready |= set(fresh)
        fresh += [SPARE] * (3 - len(fresh))
        first = sum(block << 4 * at for at, block in enumerate(blocks)) + (slot << 20) + (half << 24) + (present << 25)
        codes.append((first, sum(block << 4 * at for at, block in enumerate(fresh))))
    return codes


def by_row(lat, values):
    middle = values[LAT // 2]
    result = jnp.int32(middle)
    for row, value in enumerate(values):
        if value != middle:
            result = jnp.where(lat == row, value, result)
    return result


def positions(angles, radius):
    cosine, sine = jnp.cos(angles), jnp.sin(angles)
    ring = radius * cosine[0:1]
    return ring * cosine[1:2], ring * sine[1:2], radius * sine[0:1]


def thirds(value):
    high = value.astype(jnp.bfloat16).astype(jnp.float32)
    rest = value - high
    middle = rest.astype(jnp.bfloat16).astype(jnp.float32)
    return high, middle, rest - middle


def fill(slabs, parts, squares, flipped):
    high, middle, low = parts
    order = (high, middle, high, low, middle, high) if flipped else (high, high, middle, high, middle, low)
    for row, part in enumerate(order):
        slabs[3 * row : 3 * row + 3, :] = part
    ones = jnp.ones_like(squares[0])
    tail = (ones, ones, ones) + squares if flipped else squares + (ones, ones, ones)
    for row, part in enumerate(tail):
        slabs[18 + row : 19 + row, :] = part


def couple(squared, points, sources):
    inverse = lax.rsqrt(squared)
    second = inverse * inverse
    third = inverse * second
    fifth = third * second
    along = fifth - third
    across = fifth - third * (1.0 / 3.0)
    return [along * p - across * s for p, s in zip(points, sources)]


def prepare_source(raw, centre, slab, features, wide):
    local = raw[0:3, :] - centre
    scaled = local * (-2.0 / EDGE)
    square = jnp.sum(local * local, axis=0, keepdims=True) * (1.0 / EDGE)
    fill(slab, thirds(scaled), thirds(square), True)
    slab[24:28, :] = raw[0:4, :]
    slab[28:32, :] = jnp.zeros((4, BS), jnp.float32)
    columns = slab[...].T
    features[...] = columns.astype(jnp.bfloat16)
    for row in range(wide.shape[0]):
        column = columns[:, 24 + row : 25 + row] * (FOLD if row < 3 else 1.0)
        wide[row] = jnp.broadcast_to(column, (BS, 128))


def point_features(raw, centre, slab):
    local = raw[0:3, :] - centre
    square = jnp.sum(local * local, axis=0, keepdims=True) * (1.0 / EDGE)
    fill(slab, thirds(local), thirds(square), False)
    slab[24:32, :] = jnp.zeros((8, OBS), jnp.float32)
    return slab[...].astype(jnp.bfloat16)


def lanes_of(c, lane):
    return slice(c * HALF + lane * 128, c * HALF + lane * 128 + 128)


def exchange(count_ref, obs_ref, field_ref, dip_ref, moment_ref, dips, tiles, obs_rows, obs_features, features, wide, squared, predicted, slab_s, slab_o, send_dip, recv_dip, send_obs, recv_obs):
    lat, lon = lax.axis_index("lat"), lax.axis_index("lon")

    def inside(step):
        return (lat + step >= 0) & (lat + step < LAT)

    def device(offset):
        return (lat + offset[0], lax.rem(lon + offset[1] + LON, LON))

    barrier = pltpu.get_barrier_semaphore()
    for offset in OFFSETS[1:]:

        @pl.when(inside(offset[0]))
        def _():
            pl.semaphore_signal(barrier, inc=1, device_id=device(offset), device_id_type=pl.DeviceIdType.MESH)

    def angles(fraction):
        row = lax.broadcasted_iota(jnp.int32, fraction.shape, 0)
        index = jnp.where(row == 0, lat.astype(jnp.float32), lon.astype(jnp.float32))
        span = jnp.where(row == 0, 160.0 * DEGREE / LAT, 2.0 * math.pi / LON)
        base = jnp.where(row == 0, -80.0 * DEGREE, 0.0)
        return base + (index + fraction) * span

    for row, value in enumerate(positions(angles(dip_ref[...]), SOURCE_RADIUS)):
        dips[0, row : row + 1, :] = value
    dips[0, 3:4, :] = moment_ref[...]
    middle = positions(angles(jnp.full((2, BS), 0.5, jnp.float32)), 0.5 * (OBS_RADIUS + SOURCE_RADIUS))
    for row, value in enumerate(middle):
        dips[0, 4 + row : 5 + row, :] = value
    dips[0, 7:8, :] = jnp.zeros((1, BS), jnp.float32)

    pl.semaphore_wait(barrier, sum(inside(offset[0]).astype(jnp.int32) for offset in OFFSETS[1:]))

    def dip_copy(slot):
        step = OFFSETS[slot]
        return pltpu.make_async_remote_copy(
            src_ref=dips.at[0],
            dst_ref=dips.at[slot],
            send_sem=send_dip.at[slot],
            recv_sem=recv_dip.at[slot],
            device_id=device((-step[0], -step[1])),
            device_id_type=pl.DeviceIdType.MESH,
        )

    def obs_copy(slot):
        return pltpu.make_async_remote_copy(
            src_ref=tiles.at[0],
            dst_ref=tiles.at[slot],
            send_sem=send_obs.at[slot],
            recv_sem=recv_obs.at[slot],
            device_id=device(CROSS[slot]),
            device_id_type=pl.DeviceIdType.MESH,
        )

    for slot in range(1, len(OFFSETS)):

        @pl.when(inside(-OFFSETS[slot][0]))
        def _():
            dip_copy(slot).start()

    def dip_arrival(slot):
        @pl.when(inside(OFFSETS[slot][0]))
        def _():
            dip_copy(slot).wait_recv()

        @pl.when(jnp.logical_not(inside(OFFSETS[slot][0])))
        def _():
            dips[slot] = jnp.zeros((8, BS), jnp.float32)

    dips[SPARE] = jnp.zeros((8, BS), jnp.float32)
    for row, value in enumerate(positions(angles(obs_ref[...]), OBS_RADIUS)):
        tiles[0, row : row + 1, :] = value
    slot_index = lax.broadcasted_iota(jnp.int32, (1, OBS), 1)
    tiles[0, 6:7, :] = jnp.where(slot_index < count_ref[0, 0], 1.0, 0.0)
    tiles[0, 7:8, :] = jnp.zeros((1, OBS), jnp.float32)
    centre = dips[0, 4:7, 0:1]
    own_features = point_features(tiles[0], centre, slab_o)
    for half in range(2):
        columns = slice(half * HALF, (half + 1) * HALF)
        obs_features[half] = own_features[:, columns]
        obs_rows[half, 0:3, :] = tiles[0, 0:3, columns] * FOLD
    predicted[...] = jnp.zeros_like(predicted)
    polar = (lat == 0) | (lat == LAT - 1)
    halves = jnp.where(polar, 2, 1)

    def predict(slot):
        prepare_source(dips[slot], centre, slab_s, features, wide)

        def one_half(half, carry):
            squared[...] = jnp.dot(features[...], obs_features[half], preferred_element_type=jnp.float32)
            for lane in range(4):
                lanes = slice(lane * 128, lane * 128 + 128)
                points = [obs_rows[half, c : c + 1, lanes] for c in range(3)]
                sums = [jnp.zeros((16, 128), jnp.float32) for c in range(3)]
                for piece in range(16):
                    rows = slice(piece * 16, piece * 16 + 16)
                    values = couple(squared[rows, lanes], points, [wide[c, rows] for c in range(3)])
                    moment = wide[3, rows]
                    for c in range(3):
                        sums[c] = sums[c] + values[c] * moment
                for c in range(3):
                    predicted[half, :, lanes_of(c, lane)] += sums[c]
            return carry

        lax.fori_loop(0, halves, one_half, 0)

    def predict_slot(slot, carry):
        predict(slot)
        return carry

    lax.fori_loop(0, 1, predict_slot, 0)
    for slot in range(1, 5):
        dip_arrival(slot)
    lax.fori_loop(1, 5, predict_slot, 0)

    for half in range(2):
        for c in range(3):
            total = jnp.sum(predicted[half, :, c * HALF : (c + 1) * HALF], axis=0, keepdims=True)
            columns = slice(half * HALF, (half + 1) * HALF)
            tiles[0, 3 + c : 4 + c, columns] = field_ref[c, :, columns] - total

    for slot in range(1, len(CROSS)):

        @pl.when(inside(CROSS[slot][0]))
        def _():
            obs_copy(slot).start()

    for slot in range(5, len(OFFSETS)):
        dip_arrival(slot)

    for slot in range(1, len(OFFSETS)):

        @pl.when(inside(-OFFSETS[slot][0]))
        def _():
            dip_copy(slot).wait_send()

    for slot in range(1, len(CROSS)):

        @pl.when(inside(-CROSS[slot][0]))
        def _():
            obs_copy(slot).wait_recv()

        @pl.when(jnp.logical_not(inside(-CROSS[slot][0])))
        def _():
            tiles[slot] = jnp.zeros((8, OBS), jnp.float32)

        @pl.when(inside(CROSS[slot][0]))
        def _():
            obs_copy(slot).wait_send()


def compute(dips, tiles, gram, rhs, codes, obs_rows, obs_features, source_features, wide, squared, low, weighted, right, total, slab_s, slab_o, out_sem):
    lat = lax.axis_index("lat")
    every = [pass_codes(row) for row in range(LAT)]
    passes = by_row(lat, [len(row) for row in every])
    for number in range(max(len(row) for row in every)):
        for field in range(2):
            codes[2 * number + field] = by_row(lat, [row[number][field] if number < len(row) else 0 for row in every])
    centre = dips[0, 4:7, 0:1]

    def source_setup(slot, slab):
        prepare_source(dips[slot], centre, slab, source_features.at[slot], wide.at[slot])

    def obs_setup(slot, carry):
        raw = tiles[slot]
        features = point_features(raw, centre, slab_o)
        scaled = raw[0:3, :] * FOLD
        weight = raw[6:7, :] * HUBER_EDGE / jnp.maximum(jnp.abs(raw[3:6, :]), HUBER_EDGE)
        for half in range(2):
            columns = slice(half * HALF, (half + 1) * HALF)
            obs_features[slot, half] = features[:, columns]
            obs_rows[slot, half, 0:3, :] = scaled[:, columns]
            obs_rows[slot, half, 3:6, :] = weight[:, columns]
            obs_rows[slot, half, 6:9, :] = raw[3:6, columns]
        return carry

    lax.fori_loop(0, 5, obs_setup, 0)
    for at in range(5):
        source_setup((codes[0] >> 4 * at) & 15, slab_s.at[at])

    total[...] = jnp.zeros_like(total)
    right[...] = jnp.zeros_like(right)

    def square_block(tile, half, source, to):
        squared[to] = jnp.dot(source_features[source], obs_features[tile, half], preferred_element_type=jnp.float32)

    def couple_block(tile, half, source, position):
        for lane in range(4):
            lanes = slice(lane * 128, lane * 128 + 128)
            points = [obs_rows[tile, half, c : c + 1, lanes] for c in range(3)]
            if position == 0:
                weight = [obs_rows[tile, half, 3 + c : 4 + c, lanes] for c in range(3)]
                residual = [obs_rows[tile, half, 6 + c : 7 + c, lanes] for c in range(3)]
            for piece in range(16):
                rows = slice(piece * 16, piece * 16 + 16)
                values = couple(squared[position % 3, rows, lanes], points, [wide[source, c, rows] for c in range(3)])
                for c in range(3):
                    low[position, rows, lanes_of(c, lane)] = values[c].astype(jnp.bfloat16)
                if position == 0:
                    sums = right[rows]
                    for c in range(3):
                        value = values[c] * weight[c]
                        weighted[rows, lanes_of(c, lane)] = value.astype(jnp.bfloat16)
                        sums = sums + value * residual[c]
                    right[rows] = sums

    def add_gram(target, position):
        product = lax.dot_general(
            weighted[...], low[position], (((1,), (1,)), ((), ())), preferred_element_type=jnp.float32
        )
        total[target] = total[target] + product

    def one_pass(number, carry):
        code = codes[2 * number]
        sources = [(code >> 4 * at) & 15 for at in range(5)]
        tile, half, blocks = (code >> 20) & 15, (code >> 24) & 1, code >> 25
        fresh = codes[2 * number + 1]
        square_block(tile, half, sources[0], 0)
        for position in range(4):
            square_block(tile, half, sources[position + 1], (position + 1) % 3)
            couple_block(tile, half, sources[position], position)
            add_gram(sources[position], position)
            if position < 3:
                source_setup((fresh >> 4 * position) & 15, slab_s.at[position])

        @pl.when(blocks == 5)
        def _():
            couple_block(tile, half, sources[4], 4)
            add_gram(sources[4], 4)

        return carry

    lax.fori_loop(0, passes, one_pass, 0)
    rhs[...] = jnp.sum(right[...].T, axis=0, keepdims=True)
    copy = pltpu.make_async_copy(total.at[pl.ds(0, 13)], gram, out_sem)
    copy.start()
    copy.wait()


def shards(obs_frac, obs_field, dipole_frac, dipole_moment, obs_count):
    vmem = pl.BlockSpec(memory_space=pltpu.VMEM)
    smem = pl.BlockSpec(memory_space=pltpu.SMEM)
    slots = len(OFFSETS) + 1
    f32, low = jnp.float32, jnp.bfloat16
    dips, tiles = pl.pallas_call(
        exchange,
        out_shape=(jax.ShapeDtypeStruct((slots, 8, BS), f32), jax.ShapeDtypeStruct((5, 8, OBS), f32)),
        in_specs=[smem, vmem, vmem, vmem, vmem],
        out_specs=(vmem, vmem),
        scratch_shapes=[
            pltpu.VMEM((2, 8, HALF), f32),
            pltpu.VMEM((2, FEATURES, HALF), low),
            pltpu.VMEM((BS, FEATURES), low),
            pltpu.VMEM((4, BS, 128), f32),
            pltpu.VMEM((BS, HALF), f32),
            pltpu.VMEM((2, 16, 3 * HALF), f32),
            pltpu.VMEM((FEATURES, BS), f32),
            pltpu.VMEM((FEATURES, OBS), f32),
            pltpu.SemaphoreType.DMA((len(OFFSETS),)),
            pltpu.SemaphoreType.DMA((len(OFFSETS),)),
            pltpu.SemaphoreType.DMA((len(CROSS),)),
            pltpu.SemaphoreType.DMA((len(CROSS),)),
        ],
        compiler_params=pltpu.CompilerParams(
            collective_id=0, has_side_effects=True, vmem_limit_bytes=60 * 2**20
        ),
        name="exchange",
    )(obs_count, obs_frac[0, 0], jnp.transpose(obs_field[0], (1, 0, 2)), dipole_frac[0, 0], dipole_moment[0])
    gram, rhs = compute_call(dips, tiles)
    return gram[None, None], rhs[None]


def compute_call(dips, tiles):
    vmem = pl.BlockSpec(memory_space=pltpu.VMEM)
    slots = len(OFFSETS) + 1
    f32, low = jnp.float32, jnp.bfloat16
    return pl.pallas_call(
        compute,
        out_shape=(jax.ShapeDtypeStruct((13, BS, BS), f32), jax.ShapeDtypeStruct((1, BS), f32)),
        in_specs=[vmem, vmem],
        out_specs=(pl.BlockSpec(memory_space=pl.ANY), vmem),
        scratch_shapes=[
            pltpu.SMEM((16,), jnp.int32),
            pltpu.VMEM((5, 2, 16, HALF), f32),
            pltpu.VMEM((5, 2, FEATURES, HALF), low),
            pltpu.VMEM((slots, BS, FEATURES), low),
            pltpu.VMEM((slots, 3, BS, 128), f32),
            pltpu.VMEM((3, BS, HALF), f32),
            pltpu.VMEM((5, BS, 3 * HALF), low),
            pltpu.VMEM((BS, 3 * HALF), low),
            pltpu.VMEM((BS, 128), f32),
            pltpu.VMEM((slots, BS, BS), f32),
            pltpu.VMEM((5, FEATURES, BS), f32),
            pltpu.VMEM((FEATURES, OBS), f32),
            pltpu.SemaphoreType.DMA,
        ],
        compiler_params=pltpu.CompilerParams(vmem_limit_bytes=60 * 2**20),
        name="normal_blocks",
    )(dips, tiles)


def solution(mesh):
    in_specs = (
        P("lat", "lon", None, None),
        P("lat", "lon", None, None),
        P("lat", "lon", None, None),
        P("lat", "lon", None),
        P("lat", "lon"),
    )
    out_specs = (P("lat", "lon", None, None, None), P("lat", "lon", None))
    return jax.shard_map(shards, mesh=mesh, in_specs=in_specs, out_specs=out_specs, check_vma=False)
```

```python
import functools
import math

import jax
import jax.numpy as jnp
import numpy as np
from jax import lax
from jax.experimental import pallas as pl
from jax.experimental.pallas import tpu as pltpu
from jax.sharding import PartitionSpec as P

CROSS = ((0, 0), (-1, 0), (1, 0), (0, -1), (0, 1))
OFFSETS = (
    (0, 0),
    (-1, 0),
    (1, 0),
    (0, -1),
    (0, 1),
    (-2, 0),
    (2, 0),
    (0, -2),
    (0, 2),
    (-1, -1),
    (-1, 1),
    (1, -1),
    (1, 1),
)
OBS_RADIUS = 1.06
SOURCE_RADIUS = 0.99
KERNEL_SCALE = 0.0001
HUBER_EDGE = 0.8
DEGREE = math.pi / 180.0
LAT = 16
LON = 16
BS = 256
OBS = 1024
HALF = 512
SPARE = 13
STEPS = 22
UNROLL = 4
LAST = (3, 7)
EDGE = (1.5 * (OBS_RADIUS**2 + SOURCE_RADIUS**2) - 3.0 * SOURCE_RADIUS**2) / 1.5
FOLD = 1.5 * KERNEL_SCALE * EDGE**-1.5
FEATURES = 32


def pass_rows(lat):
    rows = []
    for slot, (lat_step, lon_step) in enumerate(CROSS):
        tile = lat - lat_step
        if not 0 <= tile < LAT:
            continue
        there = [b for b in CROSS if 0 <= tile + b[0] < LAT and b != (lat_step, lon_step)]
        there.sort(key=lambda b: b[0] == 0)
        blocks = [OFFSETS.index((b[0] - lat_step, b[1] - lon_step)) for b in there]
        for half in range(2 if tile in (0, LAT - 1) else 1):
            rows.append((slot, half, blocks))
    return rows


def step_codes(lat):
    rows = pass_rows(lat)
    first = [slot + (half << 4) for slot, half, blocks in rows]
    rest = [
        slot + (half << 4) + (number << 8) + (block << 12) + (block << 16)
        for number, (slot, half, blocks) in enumerate(rows)
        for block in blocks
    ]
    return first, [SPARE << 16] * (STEPS - len(rest)) + rest


def by_row(lat, values):
    middle = values[LAT // 2]
    result = jnp.int32(middle)
    for row, value in enumerate(values):
        if value != middle:
            result = jnp.where(lat == row, value, result)
    return result


def positions(angles, radius):
    cosine, sine = jnp.cos(angles), jnp.sin(angles)
    ring = radius * cosine[0:1]
    return ring * cosine[1:2], ring * sine[1:2], radius * sine[0:1]


def thirds(value):
    high = value.astype(jnp.bfloat16).astype(jnp.float32)
    rest = value - high
    middle = rest.astype(jnp.bfloat16).astype(jnp.float32)
    return high, middle, rest - middle


def fill(slabs, parts, squares, flipped):
    high, middle, low = parts
    order = (high, middle, high, low, middle, high) if flipped else (high, high, middle, high, middle, low)
    for row, part in enumerate(order):
        slabs[3 * row : 3 * row + 3, :] = part
    ones = jnp.ones_like(squares[0])
    tail = (ones, ones, ones) + squares if flipped else squares + (ones, ones, ones)
    for row, part in enumerate(tail):
        slabs[18 + row : 19 + row, :] = part


def couple(squared, points, sources):
    inverse = lax.rsqrt(squared)
    second = inverse * inverse
    third = inverse * second
    fifth = third * second
    along = fifth - third
    across = fifth - third * (1.0 / 3.0)
    return [along * p - across * s for p, s in zip(points, sources)]


def prepare_source(raw, centre, slab, features, wide):
    local = raw[0:3, :] - centre
    scaled = local * (-2.0 / EDGE)
    square = jnp.sum(local * local, axis=0, keepdims=True) * (1.0 / EDGE)
    fill(slab, thirds(scaled), thirds(square), True)
    slab[24:28, :] = raw[0:4, :]
    slab[28:32, :] = jnp.zeros((4, BS), jnp.float32)
    columns = slab[...].T
    features[...] = columns.astype(jnp.bfloat16)
    for row in range(wide.shape[0]):
        column = columns[:, 24 + row : 25 + row] * (FOLD if row < 3 else 1.0)
        wide[row] = jnp.broadcast_to(column, (BS, 128))


def point_features(raw, centre, slab):
    local = raw[0:3, :] - centre
    square = jnp.sum(local * local, axis=0, keepdims=True) * (1.0 / EDGE)
    fill(slab, thirds(local), thirds(square), False)
    slab[24:32, :] = jnp.zeros((8, OBS), jnp.float32)
    return slab[...].astype(jnp.bfloat16)


def lanes_of(c, lane):
    start = (lane // 2) * 768 + c * 256 + (lane % 2) * 128
    return slice(start, start + 128)


def rows_of_field(c, lane):
    return slice(c * HALF + lane * 128, c * HALF + lane * 128 + 128)


def exchange(count_ref, obs_ref, field_ref, dip_ref, moment_ref, dips, tiles, obs_rows, obs_features, features, wide, squared, predicted, slab_s, slab_o, send_dip, recv_dip, send_obs, recv_obs):
    lat, lon = lax.axis_index("lat"), lax.axis_index("lon")

    def inside(step):
        return (lat + step >= 0) & (lat + step < LAT)

    def device(offset):
        return (lat + offset[0], lax.rem(lon + offset[1] + LON, LON))

    barrier = pltpu.get_barrier_semaphore()
    for offset in OFFSETS[1:]:

        @pl.when(inside(offset[0]))
        def _():
            pl.semaphore_signal(barrier, inc=1, device_id=device(offset), device_id_type=pl.DeviceIdType.MESH)

    def angles(fraction):
        row = lax.broadcasted_iota(jnp.int32, fraction.shape, 0)
        index = jnp.where(row == 0, lat.astype(jnp.float32), lon.astype(jnp.float32))
        span = jnp.where(row == 0, 160.0 * DEGREE / LAT, 2.0 * math.pi / LON)
        base = jnp.where(row == 0, -80.0 * DEGREE, 0.0)
        return base + (index + fraction) * span

    for row, value in enumerate(positions(angles(dip_ref[...]), SOURCE_RADIUS)):
        dips[0, row : row + 1, :] = value
    dips[0, 3:4, :] = moment_ref[...]
    middle = positions(angles(jnp.full((2, BS), 0.5, jnp.float32)), 0.5 * (OBS_RADIUS + SOURCE_RADIUS))
    for row, value in enumerate(middle):
        dips[0, 4 + row : 5 + row, :] = value
    dips[0, 7:8, :] = jnp.zeros((1, BS), jnp.float32)

    pl.semaphore_wait(barrier, sum(inside(offset[0]).astype(jnp.int32) for offset in OFFSETS[1:]))

    def dip_copy(slot):
        step = OFFSETS[slot]
        return pltpu.make_async_remote_copy(
            src_ref=dips.at[0],
            dst_ref=dips.at[slot],
            send_sem=send_dip.at[slot],
            recv_sem=recv_dip.at[slot],
            device_id=device((-step[0], -step[1])),
            device_id_type=pl.DeviceIdType.MESH,
        )

    def obs_copy(slot):
        return pltpu.make_async_remote_copy(
            src_ref=tiles.at[0],
            dst_ref=tiles.at[slot],
            send_sem=send_obs.at[slot],
            recv_sem=recv_obs.at[slot],
            device_id=device(CROSS[slot]),
            device_id_type=pl.DeviceIdType.MESH,
        )

    for slot in range(1, len(OFFSETS)):

        @pl.when(inside(-OFFSETS[slot][0]))
        def _():
            dip_copy(slot).start()

    def dip_arrival(slot):
        @pl.when(inside(OFFSETS[slot][0]))
        def _():
            dip_copy(slot).wait_recv()

        @pl.when(jnp.logical_not(inside(OFFSETS[slot][0])))
        def _():
            dips[slot] = jnp.zeros((8, BS), jnp.float32)

    dips[SPARE] = jnp.zeros((8, BS), jnp.float32)
    for row, value in enumerate(positions(angles(obs_ref[...]), OBS_RADIUS)):
        tiles[0, row : row + 1, :] = value
    slot_index = lax.broadcasted_iota(jnp.int32, (1, OBS), 1)
    tiles[0, 6:7, :] = jnp.where(slot_index < count_ref[0, 0], 1.0, 0.0)
    tiles[0, 7:8, :] = jnp.zeros((1, OBS), jnp.float32)
    centre = dips[0, 4:7, 0:1]
    own_features = point_features(tiles[0], centre, slab_o)
    for half in range(2):
        columns = slice(half * HALF, (half + 1) * HALF)
        obs_features[half] = own_features[:, columns]
        obs_rows[half, 0:3, :] = tiles[0, 0:3, columns] * FOLD
    predicted[...] = jnp.zeros_like(predicted)
    polar = (lat == 0) | (lat == LAT - 1)
    halves = jnp.where(polar, 2, 1)

    def prepare(slot, to):
        prepare_source(dips[slot], centre, slab_s, features.at[to], wide.at[to])

    def predict(at, half):
        squared[...] = jnp.dot(features[at], obs_features[half], preferred_element_type=jnp.float32)
        for lane in range(4):
            lanes = slice(lane * 128, lane * 128 + 128)
            points = [obs_rows[half, c : c + 1, lanes] for c in range(3)]
            sums = [jnp.zeros((16, 128), jnp.float32) for c in range(3)]
            for piece in range(16):
                rows = slice(piece * 16, piece * 16 + 16)
                values = couple(squared[rows, lanes], points, [wide[at, c, rows] for c in range(3)])
                moment = wide[at, 3, rows]
                for c in range(3):
                    sums[c] = sums[c] + values[c] * moment
            for c in range(3):
                predicted[half, :, rows_of_field(c, lane)] += sums[c]

    def predict_own(half, carry):
        predict(0, half)
        return carry

    prepare(0, 0)
    lax.fori_loop(0, halves, predict_own, 0)
    for slot in range(1, 5):
        dip_arrival(slot)

    third = jnp.where(lat == 0, 2, 1)

    def neighbour(turn):
        return jnp.where(turn == 0, 3, jnp.where(turn == 1, 4, jnp.where(turn == 2, third, 2)))

    prepare(3, 0)

    def predict_neighbour(turn, carry):
        now = lax.rem(turn, 2)

        def one_half(half, carry):
            predict(now, half)
            prepare(neighbour(turn + 1), 1 - now)
            return carry

        return lax.fori_loop(0, halves, one_half, carry)

    lax.fori_loop(0, jnp.where(polar, 3, 4), predict_neighbour, 0)

    for half in range(2):
        for c in range(3):
            total = jnp.sum(predicted[half, :, c * HALF : (c + 1) * HALF], axis=0, keepdims=True)
            columns = slice(half * HALF, (half + 1) * HALF)
            tiles[0, 3 + c : 4 + c, columns] = field_ref[c, :, columns] - total

    for slot in range(1, len(CROSS)):

        @pl.when(inside(CROSS[slot][0]))
        def _():
            obs_copy(slot).start()

    for slot in range(5, len(OFFSETS)):
        dip_arrival(slot)

    for slot in range(1, len(OFFSETS)):

        @pl.when(inside(-OFFSETS[slot][0]))
        def _():
            dip_copy(slot).wait_send()

    for slot in range(1, len(CROSS)):

        @pl.when(inside(-CROSS[slot][0]))
        def _():
            obs_copy(slot).wait_recv()

        @pl.when(jnp.logical_not(inside(-CROSS[slot][0])))
        def _():
            tiles[slot] = jnp.zeros((8, OBS), jnp.float32)

        @pl.when(inside(CROSS[slot][0]))
        def _():
            obs_copy(slot).wait_send()


def compute(dips, tiles, gram, rhs, codes, obs_rows, obs_features, source_features, wide, squared, low_a, low_b, weighted, right, total, slab_s, slab_o, out_sem):
    lat = lax.axis_index("lat")
    every = [step_codes(row) for row in range(LAT)]
    passes = by_row(lat, [len(first) for first, rest in every])
    for part, base in ((0, 0), (1, 8)):
        for number in range(max(len(row[part]) for row in every)):
            codes[base + number] = by_row(lat, [row[part][number] if number < len(row[part]) else 0 for row in every])
    centre = dips[0, 4:7, 0:1]

    def source_setup(slot, slab):
        prepare_source(dips[slot], centre, slab, source_features.at[slot], wide.at[slot])

    def obs_setup(slot, carry):
        raw = tiles[slot]
        features = point_features(raw, centre, slab_o)
        scaled = raw[0:3, :] * FOLD
        weight = raw[6:7, :] * HUBER_EDGE / jnp.maximum(jnp.abs(raw[3:6, :]), HUBER_EDGE)
        for half in range(2):
            columns = slice(half * HALF, (half + 1) * HALF)
            obs_features[slot, half] = features[:, columns]
            obs_rows[slot, half, 0:3, :] = scaled[:, columns]
            obs_rows[slot, half, 3:6, :] = weight[:, columns]
            obs_rows[slot, half, 6:9, :] = raw[3:6, columns]
        return carry

    lax.fori_loop(0, 5, obs_setup, 0)
    source_setup(0, slab_s.at[0])
    for slot in range(1, 3):
        source_setup(slot, slab_s.at[slot])

    total[...] = jnp.zeros_like(total)
    right[...] = jnp.zeros_like(right)

    def square(tile, half, source, to):
        squared[to] = jnp.dot(source_features[source], obs_features[tile, half], preferred_element_type=jnp.float32)

    def add_gram(target, number, low):
        product = lax.dot_general(
            weighted[number], low[...], (((1,), (1,)), ((), ())), preferred_element_type=jnp.float32
        )
        total[target] = total[target] + product

    def own_square(number, to):
        code = codes[number]
        square(code & 15, (code >> 4) & 15, 0, to)

    def own_couple(number, at, low):
        code = codes[number]
        tile, half = code & 15, (code >> 4) & 15
        for lane in range(4):
            lanes = slice(lane * 128, lane * 128 + 128)
            rows_of = [obs_rows[tile, half, c : c + 1, lanes] for c in range(9)]
            for piece in range(16):
                rows = slice(piece * 16, piece * 16 + 16)
                values = couple(squared[at, rows, lanes], rows_of[0:3], [wide[0, c, rows] for c in range(3)])
                sums = right[rows]
                for c in range(3):
                    low[rows, lanes_of(c, lane)] = values[c].astype(jnp.bfloat16)
                    value = values[c] * rows_of[3 + c]
                    weighted[number, rows, lanes_of(c, lane)] = value.astype(jnp.bfloat16)
                    sums = sums + value * rows_of[6 + c]
                right[rows] = sums

    own_square(0, 0)
    buffers = (low_a, low_b)
    for number in range(5):
        if number < 4:
            own_square(number + 1, (number + 1) % 2)
        if number > 0:
            add_gram(0, number - 1, buffers[(number - 1) % 2])
        own_couple(number, number % 2, buffers[number % 2])
        for piece in range(2):
            source_setup(3 + 2 * number + piece, slab_s.at[piece])
    add_gram(0, 4, buffers[0])

    def more_own(number, carry):
        own_square(number, 0)
        own_couple(number, 0, low_a)
        add_gram(0, number, low_a)
        return carry

    lax.fori_loop(5, passes, more_own, 0)

    def decode(step):
        code = codes[8 + step]
        return code & 15, (code >> 4) & 15, (code >> 8) & 15, (code >> 12) & 15, code >> 16

    def square_step(step, to):
        tile, half, number, source, target = decode(step)
        square(tile, half, source, to)

    def couple_step(step, at, low):
        tile, half, number, source, target = decode(step)
        for lane in range(4):
            lanes = slice(lane * 128, lane * 128 + 128)
            points = [obs_rows[tile, half, c : c + 1, lanes] for c in range(3)]
            for piece in range(16):
                rows = slice(piece * 16, piece * 16 + 16)
                values = couple(squared[at, rows, lanes], points, [wide[source, c, rows] for c in range(3)])
                for c in range(3):
                    low[rows, lanes_of(c, lane)] = values[c].astype(jnp.bfloat16)

    def gram_step(step, low):
        tile, half, number, source, target = decode(step)
        add_gram(target, number, low)

    square_step(0, 0)
    square_step(1, 1)
    couple_step(0, 0, low_a)

    def steps_from(start, count):
        for ahead in range(count):
            step = start + ahead
            before, after = (low_a, low_b) if ahead % 2 == 0 else (low_b, low_a)
            square_step(step + 2, ahead % 2)
            gram_step(step, before)
            couple_step(step + 1, (ahead + 1) % 2, after)

    def some_steps(group, carry):
        steps_from(UNROLL * group, UNROLL)
        return carry

    lax.fori_loop(0, (STEPS - 2) // UNROLL, some_steps, 0)
    def out_copy(first, count, at):
        blocks = pl.ds(first, count)
        return pltpu.make_async_copy(total.at[blocks], gram.at[blocks], out_sem.at[at])

    early = [out_copy(0, 3, 0), out_copy(4, 3, 1), out_copy(8, 5, 2)]
    late = [out_copy(block, 1, 3 + at) for at, block in enumerate(LAST)]
    for copy in early:
        copy.start()
    gram_step(STEPS - 2, low_a)
    late[0].start()
    couple_step(STEPS - 1, 1, low_b)
    gram_step(STEPS - 1, low_b)
    late[1].start()
    rhs[...] = jnp.sum(right[...].T, axis=0, keepdims=True)
    for copy in early + late:
        copy.wait()


def shards(obs_frac, obs_field, dipole_frac, dipole_moment, obs_count):
    vmem = pl.BlockSpec(memory_space=pltpu.VMEM)
    smem = pl.BlockSpec(memory_space=pltpu.SMEM)
    slots = len(OFFSETS) + 1
    f32, low = jnp.float32, jnp.bfloat16
    dips, tiles = pl.pallas_call(
        exchange,
        out_shape=(jax.ShapeDtypeStruct((slots, 8, BS), f32), jax.ShapeDtypeStruct((5, 8, OBS), f32)),
        in_specs=[smem, vmem, vmem, vmem, vmem],
        out_specs=(vmem, vmem),
        scratch_shapes=[
            pltpu.VMEM((2, 8, HALF), f32),
            pltpu.VMEM((2, FEATURES, HALF), low),
            pltpu.VMEM((2, BS, FEATURES), low),
            pltpu.VMEM((2, 4, BS, 128), f32),
            pltpu.VMEM((BS, HALF), f32),
            pltpu.VMEM((2, 16, 3 * HALF), f32),
            pltpu.VMEM((FEATURES, BS), f32),
            pltpu.VMEM((FEATURES, OBS), f32),
            pltpu.SemaphoreType.DMA((len(OFFSETS),)),
            pltpu.SemaphoreType.DMA((len(OFFSETS),)),
            pltpu.SemaphoreType.DMA((len(CROSS),)),
            pltpu.SemaphoreType.DMA((len(CROSS),)),
        ],
        compiler_params=pltpu.CompilerParams(
            collective_id=0, has_side_effects=True, vmem_limit_bytes=60 * 2**20
        ),
        name="exchange",
    )(obs_count, obs_frac[0, 0], jnp.transpose(obs_field[0], (1, 0, 2)), dipole_frac[0, 0], dipole_moment[0])
    gram, rhs = compute_call(dips, tiles)
    return gram[None, None], rhs[None]


def compute_call(dips, tiles):
    vmem = pl.BlockSpec(memory_space=pltpu.VMEM)
    slots = len(OFFSETS) + 1
    f32, low = jnp.float32, jnp.bfloat16
    return pl.pallas_call(
        compute,
        out_shape=(jax.ShapeDtypeStruct((13, BS, BS), f32), jax.ShapeDtypeStruct((1, BS), f32)),
        in_specs=[vmem, vmem],
        out_specs=(pl.BlockSpec(memory_space=pl.ANY), vmem),
        scratch_shapes=[
            pltpu.SMEM((32,), jnp.int32),
            pltpu.VMEM((5, 2, 16, HALF), f32),
            pltpu.VMEM((5, 2, FEATURES, HALF), low),
            pltpu.VMEM((slots, BS, FEATURES), low),
            pltpu.VMEM((slots, 3, BS, 128), f32),
            pltpu.VMEM((2, BS, HALF), f32),
            pltpu.VMEM((BS, 3 * HALF), low),
            pltpu.VMEM((BS, 3 * HALF), low),
            pltpu.VMEM((7, BS, 3 * HALF), low),
            pltpu.VMEM((BS, 128), f32),
            pltpu.VMEM((slots, BS, BS), f32),
            pltpu.VMEM((3, FEATURES, BS), f32),
            pltpu.VMEM((FEATURES, OBS), f32),
            pltpu.SemaphoreType.DMA((5,)),
        ],
        compiler_params=pltpu.CompilerParams(vmem_limit_bytes=60 * 2**20),
        name="normal_blocks",
    )(dips, tiles)


def solution(mesh):
    in_specs = (
        P("lat", "lon", None, None),
        P("lat", "lon", None, None),
        P("lat", "lon", None, None),
        P("lat", "lon", None),
        P("lat", "lon"),
    )
    out_specs = (P("lat", "lon", None, None, None), P("lat", "lon", None))
    return jax.shard_map(shards, mesh=mesh, in_specs=in_specs, out_specs=out_specs, check_vma=False)
```

```python
import functools
import math

import jax
import jax.numpy as jnp
import numpy as np
from jax import lax
from jax.experimental import pallas as pl
from jax.experimental.pallas import tpu as pltpu
from jax.sharding import PartitionSpec as P

CROSS = ((0, 0), (-1, 0), (1, 0), (0, -1), (0, 1))
OFFSETS = (
    (0, 0),
    (-1, 0),
    (1, 0),
    (0, -1),
    (0, 1),
    (-2, 0),
    (2, 0),
    (0, -2),
    (0, 2),
    (-1, -1),
    (-1, 1),
    (1, -1),
    (1, 1),
)
OBS_RADIUS = 1.06
SOURCE_RADIUS = 0.99
KERNEL_SCALE = 0.0001
HUBER_EDGE = 0.8
DEGREE = math.pi / 180.0
LAT = 16
LON = 16
BS = 256
OBS = 1024
HALF = 512
SPARE = 13
STEPS = 18
UNROLL = 4
LAST = (3, 7)
EDGE = (1.5 * (OBS_RADIUS**2 + SOURCE_RADIUS**2) - 3.0 * SOURCE_RADIUS**2) / 1.5
FOLD = 1.5 * KERNEL_SCALE * EDGE**-1.5
FEATURES = 32


def pass_rows(lat):
    rows = []
    for slot, (lat_step, lon_step) in list(enumerate(CROSS))[1:]:
        tile = lat - lat_step
        if not 0 <= tile < LAT:
            continue
        there = [b for b in CROSS if 0 <= tile + b[0] < LAT and b != (lat_step, lon_step)]
        there.sort(key=lambda b: b[0] == 0)
        blocks = [OFFSETS.index((b[0] - lat_step, b[1] - lon_step)) for b in there]
        for half in range(2 if tile in (0, LAT - 1) else 1):
            rows.append((slot, half, blocks))
    return rows


def step_codes(lat):
    rows = pass_rows(lat)
    first = [slot + (half << 4) for slot, half, blocks in rows]
    rest = [
        slot + (half << 4) + (number << 8) + (block << 12) + (block << 16)
        for number, (slot, half, blocks) in enumerate(rows)
        for block in blocks
    ]
    return first, [(SPARE << 16) + 3] * (STEPS - len(rest)) + rest


def by_row(lat, values):
    middle = values[LAT // 2]
    result = jnp.int32(middle)
    for row, value in enumerate(values):
        if value != middle:
            result = jnp.where(lat == row, value, result)
    return result


def positions(angles, radius):
    cosine, sine = jnp.cos(angles), jnp.sin(angles)
    ring = radius * cosine[0:1]
    return ring * cosine[1:2], ring * sine[1:2], radius * sine[0:1]


def thirds(value):
    high = value.astype(jnp.bfloat16).astype(jnp.float32)
    rest = value - high
    middle = rest.astype(jnp.bfloat16).astype(jnp.float32)
    return high, middle, rest - middle


def fill(slabs, parts, squares, flipped):
    high, middle, low = parts
    order = (high, middle, high, low, middle, high) if flipped else (high, high, middle, high, middle, low)
    for row, part in enumerate(order):
        slabs[3 * row : 3 * row + 3, :] = part
    ones = jnp.ones_like(squares[0])
    tail = (ones, ones, ones) + squares if flipped else squares + (ones, ones, ones)
    for row, part in enumerate(tail):
        slabs[18 + row : 19 + row, :] = part


def couple(squared, points, sources):
    inverse = lax.rsqrt(squared)
    second = inverse * inverse
    third = inverse * second
    fifth = third * second
    along = fifth - third
    across = fifth - third * (1.0 / 3.0)
    return [along * p - across * s for p, s in zip(points, sources)]


def prepare_source(raw, centre, slab, features, wide):
    local = raw[0:3, :] - centre
    scaled = local * (-2.0 / EDGE)
    square = jnp.sum(local * local, axis=0, keepdims=True) * (1.0 / EDGE)
    fill(slab, thirds(scaled), thirds(square), True)
    slab[24:28, :] = raw[0:4, :]
    slab[28:32, :] = jnp.zeros((4, BS), jnp.float32)
    columns = slab[...].T
    features[...] = columns.astype(jnp.bfloat16)
    for row in range(wide.shape[0]):
        column = columns[:, 24 + row : 25 + row] * (FOLD if row < 3 else 1.0)
        wide[row] = jnp.broadcast_to(column, (BS, 128))


def point_features(raw, centre, slab):
    local = raw[0:3, :] - centre
    square = jnp.sum(local * local, axis=0, keepdims=True) * (1.0 / EDGE)
    fill(slab, thirds(local), thirds(square), False)
    slab[24:32, :] = jnp.zeros((8, HALF), jnp.float32)
    return slab[...].astype(jnp.bfloat16)


def lanes_of(c, lane):
    start = (lane // 2) * 768 + c * 256 + (lane % 2) * 128
    return slice(start, start + 128)


def rows_of_field(c, lane):
    return slice(c * HALF + lane * 128, c * HALF + lane * 128 + 128)


def exchange(count_ref, obs_ref, field_ref, dip_ref, moment_ref, dips, tiles, partial, rhs, obs_rows, obs_features, features, wide, squared, predicted, low, weighted, right, total, slab_s, slab_o, send_dip, recv_dip, send_obs, recv_obs, out_sem):
    lat, lon = lax.axis_index("lat"), lax.axis_index("lon")

    def inside(step):
        return (lat + step >= 0) & (lat + step < LAT)

    def device(offset):
        return (lat + offset[0], lax.rem(lon + offset[1] + LON, LON))

    barrier = pltpu.get_barrier_semaphore()
    for offset in OFFSETS[1:]:

        @pl.when(inside(offset[0]))
        def _():
            pl.semaphore_signal(barrier, inc=1, device_id=device(offset), device_id_type=pl.DeviceIdType.MESH)

    def angles(fraction):
        row = lax.broadcasted_iota(jnp.int32, fraction.shape, 0)
        index = jnp.where(row == 0, lat.astype(jnp.float32), lon.astype(jnp.float32))
        span = jnp.where(row == 0, 160.0 * DEGREE / LAT, 2.0 * math.pi / LON)
        base = jnp.where(row == 0, -80.0 * DEGREE, 0.0)
        return base + (index + fraction) * span

    for row, value in enumerate(positions(angles(dip_ref[...]), SOURCE_RADIUS)):
        dips[0, row : row + 1, :] = value
    dips[0, 3:4, :] = moment_ref[...]
    middle = positions(angles(jnp.full((2, BS), 0.5, jnp.float32)), 0.5 * (OBS_RADIUS + SOURCE_RADIUS))
    for row, value in enumerate(middle):
        dips[0, 4 + row : 5 + row, :] = value
    dips[0, 7:8, :] = jnp.zeros((1, BS), jnp.float32)

    pl.semaphore_wait(barrier, sum(inside(offset[0]).astype(jnp.int32) for offset in OFFSETS[1:]))

    def dip_copy(slot):
        step = OFFSETS[slot]
        return pltpu.make_async_remote_copy(
            src_ref=dips.at[0],
            dst_ref=dips.at[slot],
            send_sem=send_dip.at[slot],
            recv_sem=recv_dip.at[slot],
            device_id=device((-step[0], -step[1])),
            device_id_type=pl.DeviceIdType.MESH,
        )

    def polar(row):
        return (row == 0) | (row == LAT - 1)

    def obs_copy(slot, half):
        return pltpu.make_async_remote_copy(
            src_ref=tiles.at[0, half],
            dst_ref=tiles.at[slot, half],
            send_sem=send_obs.at[slot, half],
            recv_sem=recv_obs.at[slot, half],
            device_id=device(CROSS[slot]),
            device_id_type=pl.DeviceIdType.MESH,
        )

    for slot in range(1, len(OFFSETS)):

        @pl.when(inside(-OFFSETS[slot][0]))
        def _():
            dip_copy(slot).start()

    def dip_arrival(slot):
        @pl.when(inside(OFFSETS[slot][0]))
        def _():
            dip_copy(slot).wait_recv()

        @pl.when(jnp.logical_not(inside(OFFSETS[slot][0])))
        def _():
            dips[slot] = jnp.zeros((8, BS), jnp.float32)

    dips[SPARE] = jnp.zeros((8, BS), jnp.float32)
    place = positions(angles(obs_ref[...]), OBS_RADIUS)
    slot_index = lax.broadcasted_iota(jnp.int32, (1, OBS), 1)
    present = jnp.where(slot_index < count_ref[0, 0], 1.0, 0.0)
    centre = dips[0, 4:7, 0:1]
    for half in range(2):
        columns = slice(half * HALF, (half + 1) * HALF)
        for row, value in enumerate(place):
            tiles[0, half, row : row + 1, :] = value[:, columns]
        tiles[0, half, 6:7, :] = present[:, columns]
        tiles[0, half, 7:8, :] = jnp.zeros((1, HALF), jnp.float32)
        obs_features[half] = point_features(tiles[0, half], centre, slab_o)
        obs_rows[half, 0:3, :] = tiles[0, half, 0:3, :] * FOLD
    predicted[...] = jnp.zeros_like(predicted)
    total[...] = jnp.zeros_like(total)
    right[...] = jnp.zeros_like(right)
    halves = jnp.where(polar(lat), 2, 1)

    def prepare(slot, to):
        prepare_source(dips[slot], centre, slab_s, features.at[to], wide.at[to])

    def predict(at, half, slot):
        squared[...] = jnp.dot(features[at], obs_features[half], preferred_element_type=jnp.float32)
        for lane in range(4):
            lanes = slice(lane * 128, lane * 128 + 128)
            points = [obs_rows[half, c : c + 1, lanes] for c in range(3)]
            sums = [jnp.zeros((16, 128), jnp.float32) for c in range(3)]
            for piece in range(16):
                rows = slice(piece * 16, piece * 16 + 16)
                values = couple(squared[rows, lanes], points, [wide[at, c, rows] for c in range(3)])
                moment = wide[at, 3, rows]
                for c in range(3):
                    sums[c] = sums[c] + values[c] * moment
                    low[half, slot, rows, lanes_of(c, lane)] = values[c].astype(jnp.bfloat16)
            for c in range(3):
                predicted[half, :, rows_of_field(c, lane)] += sums[c]

    def predict_own(half, carry):
        predict(2, half, 0)
        return carry

    prepare(0, 2)
    lax.fori_loop(0, halves, predict_own, 0)
    for slot in range(1, 5):
        dip_arrival(slot)

    third = jnp.where(lat == 0, 2, 1)

    def neighbour(turn):
        return jnp.where(turn == 0, 3, jnp.where(turn == 1, 4, jnp.where(turn == 2, third, 2)))

    prepare(3, 0)

    def predict_neighbour(turn, carry):
        now = lax.rem(turn, 2)

        def one_half(half, carry):
            predict(now, half, neighbour(turn))
            prepare(neighbour(turn + 1), 1 - now)
            return carry

        return lax.fori_loop(0, halves, one_half, carry)

    lax.fori_loop(0, jnp.where(polar(lat), 3, 4), predict_neighbour, 0)

    for half in range(2):
        columns = slice(half * HALF, (half + 1) * HALF)
        for c in range(3):
            sums = jnp.sum(predicted[half, :, c * HALF : (c + 1) * HALF], axis=0, keepdims=True)
            tiles[0, half, 3 + c : 4 + c, :] = field_ref[c, :, columns] - sums

    for slot in range(1, len(CROSS)):

        @pl.when(inside(CROSS[slot][0]))
        def _():
            obs_copy(slot, 0).start()

            @pl.when(polar(lat))
            def _():
                obs_copy(slot, 1).start()

    for half in range(2):
        obs_rows[half, 3:6, :] = tiles[0, half, 6:7, :] * HUBER_EDGE / jnp.maximum(jnp.abs(tiles[0, half, 3:6, :]), HUBER_EDGE)

    def own_share(half, carry):
        squared[...] = jnp.dot(features[2], obs_features[half], preferred_element_type=jnp.float32)
        for lane in range(4):
            lanes = slice(lane * 128, lane * 128 + 128)
            points = [obs_rows[half, c : c + 1, lanes] for c in range(3)]
            weight = [obs_rows[half, 3 + c : 4 + c, lanes] for c in range(3)]
            residual = [tiles[0, half, 3 + c : 4 + c, lanes] for c in range(3)]
            for piece in range(16):
                rows = slice(piece * 16, piece * 16 + 16)
                values = couple(squared[rows, lanes], points, [wide[2, c, rows] for c in range(3)])
                sums = right[rows]
                for c in range(3):
                    value = values[c] * weight[c]
                    weighted[rows, lanes_of(c, lane)] = value.astype(jnp.bfloat16)
                    sums = sums + value * residual[c]
                right[rows] = sums

        def share(turn, inner):
            slot = jnp.where(turn == 0, 0, neighbour(turn - 1))
            product = lax.dot_general(
                weighted[...], low[half, slot], (((1,), (1,)), ((), ())), preferred_element_type=jnp.float32
            )
            total[slot] = total[slot] + product
            return inner

        return lax.fori_loop(0, jnp.where(polar(lat), 4, 5), share, carry)

    lax.fori_loop(0, halves, own_share, 0)
    rhs[...] = jnp.sum(right[...].T, axis=0, keepdims=True)
    partial_copy = pltpu.make_async_copy(total, partial, out_sem)
    partial_copy.start()

    for slot in range(5, len(OFFSETS)):
        dip_arrival(slot)

    for slot in range(1, len(OFFSETS)):

        @pl.when(inside(-OFFSETS[slot][0]))
        def _():
            dip_copy(slot).wait_send()

    for slot in range(1, len(CROSS)):
        step = CROSS[slot][0]

        @pl.when(inside(-step))
        def _():
            obs_copy(slot, 0).wait_recv()

            @pl.when(polar(lat - step))
            def _():
                obs_copy(slot, 1).wait_recv()

        @pl.when(inside(step))
        def _():
            obs_copy(slot, 0).wait_send()

            @pl.when(polar(lat))
            def _():
                obs_copy(slot, 1).wait_send()

    partial_copy.wait()


def compute(dips, tiles, partial, share, gram, rhs, codes, obs_rows, obs_features, source_features, wide, squared, low_a, low_b, weighted, right, total, slab_s, slab_o, out_sem, in_sem):
    lat = lax.axis_index("lat")
    every = [step_codes(row) for row in range(LAT)]
    passes = by_row(lat, [len(first) for first, rest in every])
    for part, base in ((0, 0), (1, 8)):
        for number in range(max(len(row[part]) for row in every)):
            codes[base + number] = by_row(lat, [row[part][number] if number < len(row[part]) else 0 for row in every])
    partial_copy = pltpu.make_async_copy(partial, total.at[pl.ds(0, 5)], in_sem)
    partial_copy.start()
    centre = dips[0, 4:7, 0:1]

    def source_setup(slot, slab):
        prepare_source(dips[slot], centre, slab, source_features.at[slot], wide.at[slot])

    def obs_setup(slot, carry):
        for half in range(2):
            raw = tiles[slot, half]
            obs_features[slot, half] = point_features(raw, centre, slab_o)
            obs_rows[slot, half, 0:3, :] = raw[0:3, :] * FOLD
            obs_rows[slot, half, 3:6, :] = raw[6:7, :] * HUBER_EDGE / jnp.maximum(jnp.abs(raw[3:6, :]), HUBER_EDGE)
            obs_rows[slot, half, 6:9, :] = raw[3:6, :]
        return carry

    lax.fori_loop(1, 5, obs_setup, 0)
    source_setup(0, slab_s.at[0])
    for slot in range(1, 3):
        source_setup(slot, slab_s.at[slot])

    total[5:] = jnp.zeros_like(total[5:])
    right[...] = jnp.zeros_like(right)

    def square(tile, half, source, to):
        squared[to] = jnp.dot(source_features[source], obs_features[tile, half], preferred_element_type=jnp.float32)

    def add_gram(target, number, low):
        product = lax.dot_general(
            weighted[number], low[...], (((1,), (1,)), ((), ())), preferred_element_type=jnp.float32
        )
        total[target] = total[target] + product

    def own_square(number, to):
        code = codes[number]
        square(code & 15, (code >> 4) & 15, 0, to)

    def own_couple(number, at, low):
        code = codes[number]
        tile, half = code & 15, (code >> 4) & 15
        for lane in range(4):
            lanes = slice(lane * 128, lane * 128 + 128)
            rows_of = [obs_rows[tile, half, c : c + 1, lanes] for c in range(9)]
            for piece in range(16):
                rows = slice(piece * 16, piece * 16 + 16)
                values = couple(squared[at, rows, lanes], rows_of[0:3], [wide[0, c, rows] for c in range(3)])
                sums = right[rows]
                for c in range(3):
                    low[rows, lanes_of(c, lane)] = values[c].astype(jnp.bfloat16)
                    value = values[c] * rows_of[3 + c]
                    weighted[number, rows, lanes_of(c, lane)] = value.astype(jnp.bfloat16)
                    sums = sums + value * rows_of[6 + c]
                right[rows] = sums

    own_square(0, 0)
    buffers = (low_a, low_b)
    fresh = 3
    for number in range(4):
        if number < 3:
            own_square(number + 1, (number + 1) % 2)
        if number == 1:
            partial_copy.wait()
        if number > 0:
            add_gram(0, number - 1, buffers[(number - 1) % 2])
        own_couple(number, number % 2, buffers[number % 2])
        for piece in range(3 if number < 2 else 2):
            source_setup(fresh, slab_s.at[piece])
            fresh += 1
    add_gram(0, 3, buffers[1])

    def more_own(number, carry):
        own_square(number, 0)
        own_couple(number, 0, low_a)
        add_gram(0, number, low_a)
        return carry

    lax.fori_loop(4, passes, more_own, 0)

    def decode(step):
        code = codes[8 + step]
        return code & 15, (code >> 4) & 15, (code >> 8) & 15, (code >> 12) & 15, code >> 16

    def square_step(step, to):
        tile, half, number, source, target = decode(step)
        square(tile, half, source, to)

    def couple_step(step, at, low):
        tile, half, number, source, target = decode(step)
        for lane in range(4):
            lanes = slice(lane * 128, lane * 128 + 128)
            points = [obs_rows[tile, half, c : c + 1, lanes] for c in range(3)]
            for piece in range(16):
                rows = slice(piece * 16, piece * 16 + 16)
                values = couple(squared[at, rows, lanes], points, [wide[source, c, rows] for c in range(3)])
                for c in range(3):
                    low[rows, lanes_of(c, lane)] = values[c].astype(jnp.bfloat16)

    def gram_step(step, low):
        tile, half, number, source, target = decode(step)
        add_gram(target, number, low)

    square_step(0, 0)
    square_step(1, 1)
    couple_step(0, 0, low_a)

    def steps_from(start, count):
        for ahead in range(count):
            step = start + ahead
            before, after = (low_a, low_b) if ahead % 2 == 0 else (low_b, low_a)
            square_step(step + 2, ahead % 2)
            gram_step(step, before)
            couple_step(step + 1, (ahead + 1) % 2, after)

    def some_steps(group, carry):
        steps_from(UNROLL * group, UNROLL)
        return carry

    lax.fori_loop(0, (STEPS - 2) // UNROLL, some_steps, 0)
    def out_copy(first, count, at):
        blocks = pl.ds(first, count)
        return pltpu.make_async_copy(total.at[blocks], gram.at[blocks], out_sem.at[at])

    early = [out_copy(0, 3, 0), out_copy(4, 3, 1), out_copy(8, 5, 2)]
    late = [out_copy(block, 1, 3 + at) for at, block in enumerate(LAST)]
    for copy in early:
        copy.start()
    gram_step(STEPS - 2, low_a)
    late[0].start()
    couple_step(STEPS - 1, 1, low_b)
    gram_step(STEPS - 1, low_b)
    late[1].start()
    rhs[...] = share[...] + jnp.sum(right[...].T, axis=0, keepdims=True)
    for copy in early + late:
        copy.wait()


def shards(obs_frac, obs_field, dipole_frac, dipole_moment, obs_count):
    vmem = pl.BlockSpec(memory_space=pltpu.VMEM)
    smem = pl.BlockSpec(memory_space=pltpu.SMEM)
    slots = len(OFFSETS) + 1
    f32, low = jnp.float32, jnp.bfloat16
    dips, tiles, partial, share = pl.pallas_call(
        exchange,
        out_shape=(
            jax.ShapeDtypeStruct((slots, 8, BS), f32),
            jax.ShapeDtypeStruct((5, 2, 8, HALF), f32),
            jax.ShapeDtypeStruct((5, BS, BS), f32),
            jax.ShapeDtypeStruct((1, BS), f32),
        ),
        in_specs=[smem, vmem, vmem, vmem, vmem],
        out_specs=(vmem, vmem, pl.BlockSpec(memory_space=pl.ANY), vmem),
        scratch_shapes=[
            pltpu.VMEM((2, 8, HALF), f32),
            pltpu.VMEM((2, FEATURES, HALF), low),
            pltpu.VMEM((3, BS, FEATURES), low),
            pltpu.VMEM((3, 4, BS, 128), f32),
            pltpu.VMEM((BS, HALF), f32),
            pltpu.VMEM((2, 16, 3 * HALF), f32),
            pltpu.VMEM((2, 5, BS, 3 * HALF), low),
            pltpu.VMEM((BS, 3 * HALF), low),
            pltpu.VMEM((BS, 128), f32),
            pltpu.VMEM((5, BS, BS), f32),
            pltpu.VMEM((FEATURES, BS), f32),
            pltpu.VMEM((FEATURES, HALF), f32),
            pltpu.SemaphoreType.DMA((len(OFFSETS),)),
            pltpu.SemaphoreType.DMA((len(OFFSETS),)),
            pltpu.SemaphoreType.DMA((len(CROSS), 2)),
            pltpu.SemaphoreType.DMA((len(CROSS), 2)),
            pltpu.SemaphoreType.DMA,
        ],
        compiler_params=pltpu.CompilerParams(
            collective_id=0, has_side_effects=True, vmem_limit_bytes=60 * 2**20
        ),
        name="exchange",
    )(obs_count, obs_frac[0, 0], jnp.transpose(obs_field[0], (1, 0, 2)), dipole_frac[0, 0], dipole_moment[0])
    gram, rhs = compute_call(dips, tiles, partial, share)
    return gram[None, None], rhs[None]


def compute_call(dips, tiles, partial, share):
    vmem = pl.BlockSpec(memory_space=pltpu.VMEM)
    slots = len(OFFSETS) + 1
    f32, low = jnp.float32, jnp.bfloat16
    return pl.pallas_call(
        compute,
        out_shape=(jax.ShapeDtypeStruct((13, BS, BS), f32), jax.ShapeDtypeStruct((1, BS), f32)),
        in_specs=[vmem, vmem, pl.BlockSpec(memory_space=pl.ANY), vmem],
        out_specs=(pl.BlockSpec(memory_space=pl.ANY), vmem),
        scratch_shapes=[
            pltpu.SMEM((32,), jnp.int32),
            pltpu.VMEM((5, 2, 16, HALF), f32),
            pltpu.VMEM((5, 2, FEATURES, HALF), low),
            pltpu.VMEM((slots, BS, FEATURES), low),
            pltpu.VMEM((slots, 3, BS, 128), f32),
            pltpu.VMEM((2, BS, HALF), f32),
            pltpu.VMEM((BS, 3 * HALF), low),
            pltpu.VMEM((BS, 3 * HALF), low),
            pltpu.VMEM((5, BS, 3 * HALF), low),
            pltpu.VMEM((BS, 128), f32),
            pltpu.VMEM((slots, BS, BS), f32),
            pltpu.VMEM((3, FEATURES, BS), f32),
            pltpu.VMEM((FEATURES, HALF), f32),
            pltpu.SemaphoreType.DMA((5,)),
            pltpu.SemaphoreType.DMA,
        ],
        compiler_params=pltpu.CompilerParams(vmem_limit_bytes=60 * 2**20),
        name="normal_blocks",
    )(dips, tiles, partial, share)


def solution(mesh):
    in_specs = (
        P("lat", "lon", None, None),
        P("lat", "lon", None, None),
        P("lat", "lon", None, None),
        P("lat", "lon", None),
        P("lat", "lon"),
    )
    out_specs = (P("lat", "lon", None, None, None), P("lat", "lon", None))
    return jax.shard_map(shards, mesh=mesh, in_specs=in_specs, out_specs=out_specs, check_vma=False)
```

```python
import functools
import math

import jax
import jax.numpy as jnp
import numpy as np
from jax import lax
from jax.experimental import pallas as pl
from jax.experimental.pallas import tpu as pltpu
from jax.sharding import PartitionSpec as P

CROSS = ((0, 0), (-1, 0), (1, 0), (0, -1), (0, 1))
OFFSETS = (
    (0, 0),
    (-1, 0),
    (1, 0),
    (0, -1),
    (0, 1),
    (-2, 0),
    (2, 0),
    (0, -2),
    (0, 2),
    (-1, -1),
    (-1, 1),
    (1, -1),
    (1, 1),
)
OBS_RADIUS = 1.06
SOURCE_RADIUS = 0.99
KERNEL_SCALE = 0.0001
HUBER_EDGE = 0.8
DEGREE = math.pi / 180.0
LAT = 16
LON = 16
BS = 256
OBS = 1024
HALF = 512
SPARE = 13
STEPS = 18
UNROLL = 4
LAST = (3, 7)
EDGE = (1.5 * (OBS_RADIUS**2 + SOURCE_RADIUS**2) - 3.0 * SOURCE_RADIUS**2) / 1.5
FOLD = 1.5 * KERNEL_SCALE * EDGE**-1.5
FEATURES = 32


def pass_rows(lat):
    rows = []
    for slot, (lat_step, lon_step) in list(enumerate(CROSS))[1:]:
        tile = lat - lat_step
        if not 0 <= tile < LAT:
            continue
        there = [b for b in CROSS if 0 <= tile + b[0] < LAT and b != (lat_step, lon_step)]
        there.sort(key=lambda b: b[0] == 0)
        blocks = [OFFSETS.index((b[0] - lat_step, b[1] - lon_step)) for b in there]
        for half in range(2 if tile in (0, LAT - 1) else 1):
            rows.append((slot, half, blocks))
    return rows


def step_codes(lat):
    rows = pass_rows(lat)
    first = [slot + (half << 4) for slot, half, blocks in rows]
    rest = [
        slot + (half << 4) + (number << 8) + (block << 12) + (block << 16)
        for number, (slot, half, blocks) in enumerate(rows)
        for block in blocks
    ]
    return first, [(SPARE << 16) + 3] * (STEPS - len(rest)) + rest


def by_row(lat, values):
    middle = values[LAT // 2]
    result = jnp.int32(middle)
    for row, value in enumerate(values):
        if value != middle:
            result = jnp.where(lat == row, value, result)
    return result


def positions(angles, radius):
    cosine, sine = jnp.cos(angles), jnp.sin(angles)
    ring = radius * cosine[0:1]
    return ring * cosine[1:2], ring * sine[1:2], radius * sine[0:1]


def thirds(value):
    high = value.astype(jnp.bfloat16).astype(jnp.float32)
    rest = value - high
    middle = rest.astype(jnp.bfloat16).astype(jnp.float32)
    return high, middle, rest - middle


def fill(slabs, parts, squares, flipped):
    high, middle, low = parts
    order = (high, middle, high, low, middle, high) if flipped else (high, high, middle, high, middle, low)
    for row, part in enumerate(order):
        slabs[3 * row : 3 * row + 3, :] = part
    ones = jnp.ones_like(squares[0])
    tail = (ones, ones, ones) + squares if flipped else squares + (ones, ones, ones)
    for row, part in enumerate(tail):
        slabs[18 + row : 19 + row, :] = part


def couple(squared, points, sources):
    inverse = lax.rsqrt(squared)
    second = inverse * inverse
    third = inverse * second
    fifth = third * second
    along = fifth - third
    across = fifth - third * (1.0 / 3.0)
    return [along * p - across * s for p, s in zip(points, sources)]


def prepare_source(raw, centre, slab, features, wide):
    local = raw[0:3, :] - centre
    scaled = local * (-2.0 / EDGE)
    square = jnp.sum(local * local, axis=0, keepdims=True) * (1.0 / EDGE)
    fill(slab, thirds(scaled), thirds(square), True)
    slab[24:28, :] = raw[0:4, :]
    slab[28:32, :] = jnp.zeros((4, BS), jnp.float32)
    columns = slab[...].T
    features[...] = columns.astype(jnp.bfloat16)
    for row in range(wide.shape[0]):
        column = columns[:, 24 + row : 25 + row] * (FOLD if row < 3 else 1.0)
        wide[row] = jnp.broadcast_to(column, (BS, 128))


def point_features(raw, centre, slab):
    local = raw[0:3, :] - centre
    square = jnp.sum(local * local, axis=0, keepdims=True) * (1.0 / EDGE)
    fill(slab, thirds(local), thirds(square), False)
    slab[24:32, :] = jnp.zeros((8, HALF), jnp.float32)
    return slab[...].astype(jnp.bfloat16)


def lanes_of(c, lane):
    start = (lane // 2) * 768 + c * 256 + (lane % 2) * 128
    return slice(start, start + 128)


def rows_of_field(c, lane):
    return slice(c * HALF + lane * 128, c * HALF + lane * 128 + 128)


def exchange(count_ref, obs_in, field_in, dip_in, moment_in, dips, tiles, partial, rhs, obs_rows, obs_features, features, wide, squared, predicted, low, weighted, right, total, slab_s, slab_o, send_dip, recv_dip, send_obs, recv_obs, out_sem, obs_ref, field_ref, dip_ref, moment_ref, in_sem):
    lat, lon = lax.axis_index("lat"), lax.axis_index("lon")
    pairs = ((dip_in, dip_ref), (moment_in, moment_ref), (obs_in, obs_ref), (field_in, field_ref))
    loads = [pltpu.make_async_copy(source, target, in_sem.at[at]) for at, (source, target) in enumerate(pairs)]
    for load in loads:
        load.start()

    def inside(step):
        return (lat + step >= 0) & (lat + step < LAT)

    def device(offset):
        return (lat + offset[0], lax.rem(lon + offset[1] + LON, LON))

    barrier = pltpu.get_barrier_semaphore()
    for offset in OFFSETS[1:]:

        @pl.when(inside(offset[0]))
        def _():
            pl.semaphore_signal(barrier, inc=1, device_id=device(offset), device_id_type=pl.DeviceIdType.MESH)

    def angles(fraction):
        row = lax.broadcasted_iota(jnp.int32, fraction.shape, 0)
        index = jnp.where(row == 0, lat.astype(jnp.float32), lon.astype(jnp.float32))
        span = jnp.where(row == 0, 160.0 * DEGREE / LAT, 2.0 * math.pi / LON)
        base = jnp.where(row == 0, -80.0 * DEGREE, 0.0)
        return base + (index + fraction) * span

    for load in loads[:2]:
        load.wait()
    for row, value in enumerate(positions(angles(dip_ref[...]), SOURCE_RADIUS)):
        dips[0, row : row + 1, :] = value
    dips[0, 3:4, :] = moment_ref[...]
    middle = positions(angles(jnp.full((2, BS), 0.5, jnp.float32)), 0.5 * (OBS_RADIUS + SOURCE_RADIUS))
    for row, value in enumerate(middle):
        dips[0, 4 + row : 5 + row, :] = value
    dips[0, 7:8, :] = jnp.zeros((1, BS), jnp.float32)

    pl.semaphore_wait(barrier, sum(inside(offset[0]).astype(jnp.int32) for offset in OFFSETS[1:]))

    def dip_copy(slot):
        step = OFFSETS[slot]
        return pltpu.make_async_remote_copy(
            src_ref=dips.at[0],
            dst_ref=dips.at[slot],
            send_sem=send_dip.at[slot],
            recv_sem=recv_dip.at[slot],
            device_id=device((-step[0], -step[1])),
            device_id_type=pl.DeviceIdType.MESH,
        )

    def polar(row):
        return (row == 0) | (row == LAT - 1)

    def obs_copy(slot, half):
        return pltpu.make_async_remote_copy(
            src_ref=tiles.at[0, half],
            dst_ref=tiles.at[slot, half],
            send_sem=send_obs.at[slot, half],
            recv_sem=recv_obs.at[slot, half],
            device_id=device(CROSS[slot]),
            device_id_type=pl.DeviceIdType.MESH,
        )

    for slot in range(1, len(OFFSETS)):

        @pl.when(inside(-OFFSETS[slot][0]))
        def _():
            dip_copy(slot).start()

    def dip_arrival(slot):
        @pl.when(inside(OFFSETS[slot][0]))
        def _():
            dip_copy(slot).wait_recv()

        @pl.when(jnp.logical_not(inside(OFFSETS[slot][0])))
        def _():
            dips[slot] = jnp.zeros((8, BS), jnp.float32)

    dips[SPARE] = jnp.zeros((8, BS), jnp.float32)
    for load in loads[2:]:
        load.wait()
    place = positions(angles(obs_ref[...]), OBS_RADIUS)
    slot_index = lax.broadcasted_iota(jnp.int32, (1, OBS), 1)
    present = jnp.where(slot_index < count_ref[0, 0], 1.0, 0.0)
    centre = dips[0, 4:7, 0:1]
    for half in range(2):
        columns = slice(half * HALF, (half + 1) * HALF)
        for row, value in enumerate(place):
            tiles[0, half, row : row + 1, :] = value[:, columns]
        tiles[0, half, 6:7, :] = present[:, columns]
        tiles[0, half, 7:8, :] = jnp.zeros((1, HALF), jnp.float32)
        obs_features[half] = point_features(tiles[0, half], centre, slab_o)
        obs_rows[half, 0:3, :] = tiles[0, half, 0:3, :] * FOLD
    predicted[...] = jnp.zeros_like(predicted)
    total[...] = jnp.zeros_like(total)
    right[...] = jnp.zeros_like(right)
    halves = jnp.where(polar(lat), 2, 1)

    def prepare(slot, to):
        prepare_source(dips[slot], centre, slab_s, features.at[to], wide.at[to])

    def predict(at, half, slot):
        squared[...] = jnp.dot(features[at], obs_features[half], preferred_element_type=jnp.float32)
        for lane in range(4):
            lanes = slice(lane * 128, lane * 128 + 128)
            points = [obs_rows[half, c : c + 1, lanes] for c in range(3)]
            sums = [jnp.zeros((16, 128), jnp.float32) for c in range(3)]
            for piece in range(16):
                rows = slice(piece * 16, piece * 16 + 16)
                values = couple(squared[rows, lanes], points, [wide[at, c, rows] for c in range(3)])
                moment = wide[at, 3, rows]
                for c in range(3):
                    sums[c] = sums[c] + values[c] * moment
                    low[half, slot, rows, lanes_of(c, lane)] = values[c].astype(jnp.bfloat16)
            for c in range(3):
                predicted[half, :, rows_of_field(c, lane)] += sums[c]

    def predict_own(half, carry):
        predict(2, half, 0)
        return carry

    prepare(0, 2)
    lax.fori_loop(0, halves, predict_own, 0)
    for slot in range(1, 5):
        dip_arrival(slot)

    third = jnp.where(lat == 0, 2, 1)

    def neighbour(turn):
        return jnp.where(turn == 0, 3, jnp.where(turn == 1, 4, jnp.where(turn == 2, third, 2)))

    prepare(3, 0)

    def predict_neighbour(turn, carry):
        now = lax.rem(turn, 2)

        def one_half(half, carry):
            prepare(neighbour(turn + 1), 1 - now)
            predict(now, half, neighbour(turn))
            return carry

        return lax.fori_loop(0, halves, one_half, carry)

    lax.fori_loop(0, jnp.where(polar(lat), 3, 4), predict_neighbour, 0)

    for half in range(2):
        columns = slice(half * HALF, (half + 1) * HALF)
        for c in range(3):
            sums = jnp.sum(predicted[half, :, c * HALF : (c + 1) * HALF], axis=0, keepdims=True)
            tiles[0, half, 3 + c : 4 + c, :] = field_ref[c, :, columns] - sums

    for slot in range(1, len(CROSS)):

        @pl.when(inside(CROSS[slot][0]))
        def _():
            obs_copy(slot, 0).start()

            @pl.when(polar(lat))
            def _():
                obs_copy(slot, 1).start()

    for half in range(2):
        obs_rows[half, 3:6, :] = tiles[0, half, 6:7, :] * HUBER_EDGE / jnp.maximum(jnp.abs(tiles[0, half, 3:6, :]), HUBER_EDGE)

    def own_share(half, carry):
        squared[...] = jnp.dot(features[2], obs_features[half], preferred_element_type=jnp.float32)
        for lane in range(4):
            lanes = slice(lane * 128, lane * 128 + 128)
            points = [obs_rows[half, c : c + 1, lanes] for c in range(3)]
            weight = [obs_rows[half, 3 + c : 4 + c, lanes] for c in range(3)]
            residual = [tiles[0, half, 3 + c : 4 + c, lanes] for c in range(3)]
            for piece in range(16):
                rows = slice(piece * 16, piece * 16 + 16)
                values = couple(squared[rows, lanes], points, [wide[2, c, rows] for c in range(3)])
                sums = right[rows]
                for c in range(3):
                    value = values[c] * weight[c]
                    weighted[rows, lanes_of(c, lane)] = value.astype(jnp.bfloat16)
                    sums = sums + value * residual[c]
                right[rows] = sums

        def share(turn, inner):
            slot = jnp.where(turn == 0, 0, neighbour(turn - 1))
            product = lax.dot_general(
                weighted[...], low[half, slot], (((1,), (1,)), ((), ())), preferred_element_type=jnp.float32
            )
            total[slot] = total[slot] + product
            return inner

        return lax.fori_loop(0, jnp.where(polar(lat), 4, 5), share, carry)

    lax.fori_loop(0, halves, own_share, 0)
    rhs[...] = jnp.sum(right[...].T, axis=0, keepdims=True)
    partial_copy = pltpu.make_async_copy(total, partial, out_sem)
    partial_copy.start()

    for slot in range(5, len(OFFSETS)):
        dip_arrival(slot)

    for slot in range(1, len(OFFSETS)):

        @pl.when(inside(-OFFSETS[slot][0]))
        def _():
            dip_copy(slot).wait_send()

    for slot in range(1, len(CROSS)):
        step = CROSS[slot][0]

        @pl.when(inside(-step))
        def _():
            obs_copy(slot, 0).wait_recv()

            @pl.when(polar(lat - step))
            def _():
                obs_copy(slot, 1).wait_recv()

        @pl.when(inside(step))
        def _():
            obs_copy(slot, 0).wait_send()

            @pl.when(polar(lat))
            def _():
                obs_copy(slot, 1).wait_send()

    partial_copy.wait()


def compute(dips, tiles, partial, share, gram, rhs, codes, obs_rows, obs_features, source_features, wide, squared, low_a, low_b, weighted, right, total, slab_s, slab_o, out_sem, in_sem):
    lat = lax.axis_index("lat")
    every = [step_codes(row) for row in range(LAT)]
    passes = by_row(lat, [len(first) for first, rest in every])
    for part, base in ((0, 0), (1, 8)):
        for number in range(max(len(row[part]) for row in every)):
            codes[base + number] = by_row(lat, [row[part][number] if number < len(row[part]) else 0 for row in every])
    partial_copy = pltpu.make_async_copy(partial, total.at[pl.ds(0, 5)], in_sem)
    partial_copy.start()
    centre = dips[0, 4:7, 0:1]

    def source_setup(slot, slab):
        prepare_source(dips[slot], centre, slab, source_features.at[slot], wide.at[slot])

    def obs_setup(slot, carry):
        for half in range(2):
            raw = tiles[slot, half]
            obs_features[slot, half] = point_features(raw, centre, slab_o)
            obs_rows[slot, half, 0:3, :] = raw[0:3, :] * FOLD
            obs_rows[slot, half, 3:6, :] = raw[6:7, :] * HUBER_EDGE / jnp.maximum(jnp.abs(raw[3:6, :]), HUBER_EDGE)
            obs_rows[slot, half, 6:9, :] = raw[3:6, :]
        return carry

    lax.fori_loop(1, 5, obs_setup, 0)
    source_setup(0, slab_s.at[0])
    for slot in range(1, 3):
        source_setup(slot, slab_s.at[slot])

    total[5:] = jnp.zeros_like(total[5:])
    right[...] = jnp.zeros_like(right)

    def square(tile, half, source, to):
        squared[to] = jnp.dot(source_features[source], obs_features[tile, half], preferred_element_type=jnp.float32)

    def add_gram(target, number, low):
        product = lax.dot_general(
            weighted[number], low[...], (((1,), (1,)), ((), ())), preferred_element_type=jnp.float32
        )
        total[target] = total[target] + product

    def own_square(number, to):
        code = codes[number]
        square(code & 15, (code >> 4) & 15, 0, to)

    def own_couple(number, at, low):
        code = codes[number]
        tile, half = code & 15, (code >> 4) & 15
        for lane in range(4):
            lanes = slice(lane * 128, lane * 128 + 128)
            rows_of = [obs_rows[tile, half, c : c + 1, lanes] for c in range(9)]
            for piece in range(16):
                rows = slice(piece * 16, piece * 16 + 16)
                values = couple(squared[at, rows, lanes], rows_of[0:3], [wide[0, c, rows] for c in range(3)])
                sums = right[rows]
                for c in range(3):
                    low[rows, lanes_of(c, lane)] = values[c].astype(jnp.bfloat16)
                    value = values[c] * rows_of[3 + c]
                    weighted[number, rows, lanes_of(c, lane)] = value.astype(jnp.bfloat16)
                    sums = sums + value * rows_of[6 + c]
                right[rows] = sums

    own_square(0, 0)
    buffers = (low_a, low_b)
    fresh = 3
    for number in range(4):
        if number < 3:
            own_square(number + 1, (number + 1) % 2)
        if number == 1:
            partial_copy.wait()
        if number > 0:
            add_gram(0, number - 1, buffers[(number - 1) % 2])
        for piece in range(3 if number < 2 else 2):
            source_setup(fresh, slab_s.at[piece])
            fresh += 1
        own_couple(number, number % 2, buffers[number % 2])
    add_gram(0, 3, buffers[1])

    def more_own(number, carry):
        own_square(number, 0)
        own_couple(number, 0, low_a)
        add_gram(0, number, low_a)
        return carry

    lax.fori_loop(4, passes, more_own, 0)

    def decode(step):
        code = codes[8 + step]
        return code & 15, (code >> 4) & 15, (code >> 8) & 15, (code >> 12) & 15, code >> 16

    def square_step(step, to):
        tile, half, number, source, target = decode(step)
        square(tile, half, source, to)

    def couple_step(step, at, low):
        tile, half, number, source, target = decode(step)
        for lane in range(4):
            lanes = slice(lane * 128, lane * 128 + 128)
            points = [obs_rows[tile, half, c : c + 1, lanes] for c in range(3)]
            for piece in range(16):
                rows = slice(piece * 16, piece * 16 + 16)
                values = couple(squared[at, rows, lanes], points, [wide[source, c, rows] for c in range(3)])
                for c in range(3):
                    low[rows, lanes_of(c, lane)] = values[c].astype(jnp.bfloat16)

    def gram_step(step, low):
        tile, half, number, source, target = decode(step)
        add_gram(target, number, low)

    square_step(0, 0)
    square_step(1, 1)
    couple_step(0, 0, low_a)

    def steps_from(start, count):
        for ahead in range(count):
            step = start + ahead
            before, after = (low_a, low_b) if ahead % 2 == 0 else (low_b, low_a)
            square_step(step + 2, ahead % 2)
            gram_step(step, before)
            couple_step(step + 1, (ahead + 1) % 2, after)

    def some_steps(group, carry):
        steps_from(UNROLL * group, UNROLL)
        return carry

    lax.fori_loop(0, (STEPS - 2) // UNROLL, some_steps, 0)
    def out_copy(first, count, at):
        blocks = pl.ds(first, count)
        return pltpu.make_async_copy(total.at[blocks], gram.at[blocks], out_sem.at[at])

    early = [out_copy(0, 3, 0), out_copy(4, 3, 1), out_copy(8, 5, 2)]
    late = [out_copy(block, 1, 3 + at) for at, block in enumerate(LAST)]
    for copy in early:
        copy.start()
    gram_step(STEPS - 2, low_a)
    late[0].start()
    couple_step(STEPS - 1, 1, low_b)
    gram_step(STEPS - 1, low_b)
    late[1].start()
    rhs[...] = share[...] + jnp.sum(right[...].T, axis=0, keepdims=True)
    for copy in early + late:
        copy.wait()


def shards(obs_frac, obs_field, dipole_frac, dipole_moment, obs_count):
    vmem = pl.BlockSpec(memory_space=pltpu.VMEM)
    slots = len(OFFSETS) + 1
    f32, low = jnp.float32, jnp.bfloat16
    dips, tiles, partial, share = pl.pallas_call(
        exchange,
        out_shape=(
            jax.ShapeDtypeStruct((slots, 8, BS), f32),
            jax.ShapeDtypeStruct((5, 2, 8, HALF), f32),
            jax.ShapeDtypeStruct((5, BS, BS), f32),
            jax.ShapeDtypeStruct((1, BS), f32),
        ),
        in_specs=[pl.BlockSpec(memory_space=pltpu.SMEM)] + [pl.BlockSpec(memory_space=pl.ANY)] * 4,
        out_specs=(vmem, vmem, pl.BlockSpec(memory_space=pl.ANY), vmem),
        scratch_shapes=[
            pltpu.VMEM((2, 8, HALF), f32),
            pltpu.VMEM((2, FEATURES, HALF), low),
            pltpu.VMEM((3, BS, FEATURES), low),
            pltpu.VMEM((3, 4, BS, 128), f32),
            pltpu.VMEM((BS, HALF), f32),
            pltpu.VMEM((2, 16, 3 * HALF), f32),
            pltpu.VMEM((2, 5, BS, 3 * HALF), low),
            pltpu.VMEM((BS, 3 * HALF), low),
            pltpu.VMEM((BS, 128), f32),
            pltpu.VMEM((5, BS, BS), f32),
            pltpu.VMEM((FEATURES, BS), f32),
            pltpu.VMEM((FEATURES, HALF), f32),
            pltpu.SemaphoreType.DMA((len(OFFSETS),)),
            pltpu.SemaphoreType.DMA((len(OFFSETS),)),
            pltpu.SemaphoreType.DMA((len(CROSS), 2)),
            pltpu.SemaphoreType.DMA((len(CROSS), 2)),
            pltpu.SemaphoreType.DMA,
            pltpu.VMEM((2, OBS), f32),
            pltpu.VMEM((3, 1, OBS), f32),
            pltpu.VMEM((2, BS), f32),
            pltpu.VMEM((1, BS), f32),
            pltpu.SemaphoreType.DMA((4,)),
        ],
        compiler_params=pltpu.CompilerParams(
            collective_id=0, has_side_effects=True, vmem_limit_bytes=60 * 2**20
        ),
        name="exchange",
    )(obs_count, obs_frac[0, 0], jnp.transpose(obs_field[0], (1, 0, 2)), dipole_frac[0, 0], dipole_moment[0])
    gram, rhs = compute_call(dips, tiles, partial, share)
    return gram[None, None], rhs[None]


def compute_call(dips, tiles, partial, share):
    vmem = pl.BlockSpec(memory_space=pltpu.VMEM)
    slots = len(OFFSETS) + 1
    f32, low = jnp.float32, jnp.bfloat16
    return pl.pallas_call(
        compute,
        out_shape=(jax.ShapeDtypeStruct((13, BS, BS), f32), jax.ShapeDtypeStruct((1, BS), f32)),
        in_specs=[vmem, vmem, pl.BlockSpec(memory_space=pl.ANY), vmem],
        out_specs=(pl.BlockSpec(memory_space=pl.ANY), vmem),
        scratch_shapes=[
            pltpu.SMEM((32,), jnp.int32),
            pltpu.VMEM((5, 2, 16, HALF), f32),
            pltpu.VMEM((5, 2, FEATURES, HALF), low),
            pltpu.VMEM((slots, BS, FEATURES), low),
            pltpu.VMEM((slots, 3, BS, 128), f32),
            pltpu.VMEM((2, BS, HALF), f32),
            pltpu.VMEM((BS, 3 * HALF), low),
            pltpu.VMEM((BS, 3 * HALF), low),
            pltpu.VMEM((5, BS, 3 * HALF), low),
            pltpu.VMEM((BS, 128), f32),
            pltpu.VMEM((slots, BS, BS), f32),
            pltpu.VMEM((3, FEATURES, BS), f32),
            pltpu.VMEM((FEATURES, HALF), f32),
            pltpu.SemaphoreType.DMA((5,)),
            pltpu.SemaphoreType.DMA,
        ],
        compiler_params=pltpu.CompilerParams(vmem_limit_bytes=60 * 2**20),
        name="normal_blocks",
    )(dips, tiles, partial, share)


def solution(mesh):
    in_specs = (
        P("lat", "lon", None, None),
        P("lat", "lon", None, None),
        P("lat", "lon", None, None),
        P("lat", "lon", None),
        P("lat", "lon"),
    )
    out_specs = (P("lat", "lon", None, None, None), P("lat", "lon", None))
    return jax.shard_map(shards, mesh=mesh, in_specs=in_specs, out_specs=out_specs, check_vma=False)
```

```python
import functools
import math

import jax
import jax.numpy as jnp
import numpy as np
from jax import lax
from jax.experimental import pallas as pl
from jax.experimental.pallas import tpu as pltpu
from jax.sharding import PartitionSpec as P

CROSS = ((0, 0), (-1, 0), (1, 0), (0, -1), (0, 1))
OFFSETS = (
    (0, 0),
    (-1, 0),
    (1, 0),
    (0, -1),
    (0, 1),
    (-2, 0),
    (2, 0),
    (0, -2),
    (0, 2),
    (-1, -1),
    (-1, 1),
    (1, -1),
    (1, 1),
)
OBS_RADIUS = 1.06
SOURCE_RADIUS = 0.99
KERNEL_SCALE = 0.0001
HUBER_EDGE = 0.8
DEGREE = math.pi / 180.0
LAT = 16
LON = 16
BS = 256
OBS = 1024
HALF = 512
SPARE = 13
STEPS = 18
UNROLL = 4
LAST = (3, 7)
EDGE = (1.5 * (OBS_RADIUS**2 + SOURCE_RADIUS**2) - 3.0 * SOURCE_RADIUS**2) / 1.5
FOLD = 1.5 * KERNEL_SCALE * EDGE**-1.5
FEATURES = 32


def pass_rows(lat):
    rows = []
    for slot, (lat_step, lon_step) in list(enumerate(CROSS))[1:]:
        tile = lat - lat_step
        if not 0 <= tile < LAT:
            continue
        there = [b for b in CROSS if 0 <= tile + b[0] < LAT and b != (lat_step, lon_step)]
        there.sort(key=lambda b: b[0] == 0)
        blocks = [OFFSETS.index((b[0] - lat_step, b[1] - lon_step)) for b in there]
        for half in range(2 if tile in (0, LAT - 1) else 1):
            rows.append((slot, half, blocks))
    return rows


def step_codes(lat):
    rows = pass_rows(lat)
    first = [slot + (half << 4) for slot, half, blocks in rows]
    rest = [
        slot + (half << 4) + (number << 8) + (block << 12) + (block << 16)
        for number, (slot, half, blocks) in enumerate(rows)
        for block in blocks
    ]
    return first, [(SPARE << 16) + 3] * (STEPS - len(rest)) + rest


def by_row(lat, values):
    middle = values[LAT // 2]
    result = jnp.int32(middle)
    for row, value in enumerate(values):
        if value != middle:
            result = jnp.where(lat == row, value, result)
    return result


def positions(angles, radius):
    cosine, sine = jnp.cos(angles), jnp.sin(angles)
    ring = radius * cosine[0:1]
    return ring * cosine[1:2], ring * sine[1:2], radius * sine[0:1]


def thirds(value):
    high = value.astype(jnp.bfloat16).astype(jnp.float32)
    rest = value - high
    middle = rest.astype(jnp.bfloat16).astype(jnp.float32)
    return high, middle, rest - middle


def fill(slabs, parts, squares, flipped):
    high, middle, low = parts
    order = (high, middle, high, low, middle, high) if flipped else (high, high, middle, high, middle, low)
    for row, part in enumerate(order):
        slabs[3 * row : 3 * row + 3, :] = part
    ones = jnp.ones_like(squares[0])
    tail = (ones, ones, ones) + squares if flipped else squares + (ones, ones, ones)
    for row, part in enumerate(tail):
        slabs[18 + row : 19 + row, :] = part


def couple(squared, points, sources):
    inverse = lax.rsqrt(squared)
    second = inverse * inverse
    third = inverse * second
    fifth = third * second
    along = fifth - third
    across = fifth - third * (1.0 / 3.0)
    return [along * p - across * s for p, s in zip(points, sources)]


def prepare_source(raw, centre, slab, features, wide):
    local = raw[0:3, :] - centre
    scaled = local * (-2.0 / EDGE)
    square = jnp.sum(local * local, axis=0, keepdims=True) * (1.0 / EDGE)
    fill(slab, thirds(scaled), thirds(square), True)
    slab[24:28, :] = raw[0:4, :]
    slab[28:32, :] = jnp.zeros((4, BS), jnp.float32)
    columns = slab[...].T
    features[...] = columns.astype(jnp.bfloat16)
    for row in range(wide.shape[0]):
        column = columns[:, 24 + row : 25 + row] * (FOLD if row < 3 else 1.0)
        wide[row] = jnp.broadcast_to(column, (BS, 128))


def point_features(raw, centre, slab):
    local = raw[0:3, :] - centre
    square = jnp.sum(local * local, axis=0, keepdims=True) * (1.0 / EDGE)
    fill(slab, thirds(local), thirds(square), False)
    slab[24:32, :] = jnp.zeros((8, HALF), jnp.float32)
    return slab[...].astype(jnp.bfloat16)


def lanes_of(c, lane):
    start = (lane // 2) * 768 + c * 256 + (lane % 2) * 128
    return slice(start, start + 128)


def rows_of_field(c, lane):
    return slice(c * HALF + lane * 128, c * HALF + lane * 128 + 128)


def exchange(count_ref, obs_in, field_in, dip_in, moment_in, dips, tiles, partial, rhs, obs_rows, obs_features, features, wide, squared, predicted, low, weighted, right, total, slab_s, slab_o, send_dip, recv_dip, send_obs, recv_obs, out_sem, obs_ref, field_ref, dip_ref, moment_ref, in_sem):
    lat, lon = lax.axis_index("lat"), lax.axis_index("lon")
    pairs = ((dip_in, dip_ref), (moment_in, moment_ref), (obs_in, obs_ref), (field_in, field_ref))
    loads = [pltpu.make_async_copy(source, target, in_sem.at[at]) for at, (source, target) in enumerate(pairs)]
    for load in loads:
        load.start()

    def inside(step):
        return (lat + step >= 0) & (lat + step < LAT)

    def device(offset):
        return (lat + offset[0], lax.rem(lon + offset[1] + LON, LON))

    barrier = pltpu.get_barrier_semaphore()
    for offset in OFFSETS[1:]:

        @pl.when(inside(offset[0]))
        def _():
            pl.semaphore_signal(barrier, inc=1, device_id=device(offset), device_id_type=pl.DeviceIdType.MESH)

    def angles(fraction):
        row = lax.broadcasted_iota(jnp.int32, fraction.shape, 0)
        index = jnp.where(row == 0, lat.astype(jnp.float32), lon.astype(jnp.float32))
        span = jnp.where(row == 0, 160.0 * DEGREE / LAT, 2.0 * math.pi / LON)
        base = jnp.where(row == 0, -80.0 * DEGREE, 0.0)
        return base + (index + fraction) * span

    for load in loads[:2]:
        load.wait()
    for row, value in enumerate(positions(angles(dip_ref[...]), SOURCE_RADIUS)):
        dips[0, row : row + 1, :] = value
    dips[0, 3:4, :] = moment_ref[...]
    middle = positions(angles(jnp.full((2, BS), 0.5, jnp.float32)), 0.5 * (OBS_RADIUS + SOURCE_RADIUS))
    for row, value in enumerate(middle):
        dips[0, 4 + row : 5 + row, :] = value
    dips[0, 7:8, :] = jnp.zeros((1, BS), jnp.float32)

    pl.semaphore_wait(barrier, sum(inside(offset[0]).astype(jnp.int32) for offset in OFFSETS[1:]))

    def dip_copy(slot):
        step = OFFSETS[slot]
        return pltpu.make_async_remote_copy(
            src_ref=dips.at[0],
            dst_ref=dips.at[slot],
            send_sem=send_dip.at[slot],
            recv_sem=recv_dip.at[slot],
            device_id=device((-step[0], -step[1])),
            device_id_type=pl.DeviceIdType.MESH,
        )

    def polar(row):
        return (row == 0) | (row == LAT - 1)

    def obs_copy(slot, half):
        return pltpu.make_async_remote_copy(
            src_ref=tiles.at[0, half],
            dst_ref=tiles.at[slot, half],
            send_sem=send_obs.at[slot, half],
            recv_sem=recv_obs.at[slot, half],
            device_id=device(CROSS[slot]),
            device_id_type=pl.DeviceIdType.MESH,
        )

    for slot in range(1, len(OFFSETS)):

        @pl.when(inside(-OFFSETS[slot][0]))
        def _():
            dip_copy(slot).start()

    def dip_arrival(slot):
        @pl.when(inside(OFFSETS[slot][0]))
        def _():
            dip_copy(slot).wait_recv()

        @pl.when(jnp.logical_not(inside(OFFSETS[slot][0])))
        def _():
            dips[slot] = jnp.zeros((8, BS), jnp.float32)

    dips[SPARE] = jnp.zeros((8, BS), jnp.float32)
    for load in loads[2:]:
        load.wait()
    place = positions(angles(obs_ref[...]), OBS_RADIUS)
    slot_index = lax.broadcasted_iota(jnp.int32, (1, OBS), 1)
    present = jnp.where(slot_index < count_ref[0, 0], 1.0, 0.0)
    centre = dips[0, 4:7, 0:1]
    for half in range(2):
        columns = slice(half * HALF, (half + 1) * HALF)
        for row, value in enumerate(place):
            tiles[0, half, row : row + 1, :] = value[:, columns]
        tiles[0, half, 6:7, :] = present[:, columns]
        tiles[0, half, 7:8, :] = jnp.zeros((1, HALF), jnp.float32)
        obs_features[half] = point_features(tiles[0, half], centre, slab_o)
        obs_rows[half, 0:3, :] = tiles[0, half, 0:3, :] * FOLD
    predicted[...] = jnp.zeros_like(predicted)
    total[...] = jnp.zeros_like(total)
    right[...] = jnp.zeros_like(right)
    halves = jnp.where(polar(lat), 2, 1)

    def prepare(slot, to):
        prepare_source(dips[slot], centre, slab_s, features.at[to], wide.at[to])

    def predict(at, half, slot):
        squared[...] = jnp.dot(features[at], obs_features[half], preferred_element_type=jnp.float32)
        for lane in range(4):
            lanes = slice(lane * 128, lane * 128 + 128)
            points = [obs_rows[half, c : c + 1, lanes] for c in range(3)]
            sums = [jnp.zeros((16, 128), jnp.float32) for c in range(3)]
            for piece in range(16):
                rows = slice(piece * 16, piece * 16 + 16)
                values = couple(squared[rows, lanes], points, [wide[at, c, rows] for c in range(3)])
                moment = wide[at, 3, rows]
                for c in range(3):
                    sums[c] = sums[c] + values[c] * moment
                    low[half, slot, rows, lanes_of(c, lane)] = values[c].astype(jnp.bfloat16)
            for c in range(3):
                predicted[half, :, rows_of_field(c, lane)] += sums[c]

    def predict_own(half, carry):
        predict(2, half, 0)
        return carry

    prepare(0, 2)
    lax.fori_loop(0, halves, predict_own, 0)
    for slot in range(1, 5):
        dip_arrival(slot)

    third = jnp.where(lat == 0, 2, 1)

    def neighbour(turn):
        return jnp.where(turn == 0, 3, jnp.where(turn == 1, 4, jnp.where(turn == 2, third, 2)))

    prepare(3, 0)

    def predict_neighbour(turn, carry):
        now = lax.rem(turn, 2)

        def one_half(half, carry):
            prepare(neighbour(turn + 1), 1 - now)
            predict(now, half, neighbour(turn))
            return carry

        return lax.fori_loop(0, halves, one_half, carry)

    lax.fori_loop(0, jnp.where(polar(lat), 3, 4), predict_neighbour, 0)

    for half in range(2):
        columns = slice(half * HALF, (half + 1) * HALF)
        for c in range(3):
            sums = jnp.sum(predicted[half, :, c * HALF : (c + 1) * HALF], axis=0, keepdims=True)
            tiles[0, half, 3 + c : 4 + c, :] = field_ref[c, :, columns] - sums

    for slot in (3, 4, 1, 2):

        @pl.when(inside(CROSS[slot][0]))
        def _():
            obs_copy(slot, 0).start()

            @pl.when(polar(lat))
            def _():
                obs_copy(slot, 1).start()

    for half in range(2):
        obs_rows[half, 3:6, :] = tiles[0, half, 6:7, :] * HUBER_EDGE / jnp.maximum(jnp.abs(tiles[0, half, 3:6, :]), HUBER_EDGE)

    def partial_copy(slot):
        return pltpu.make_async_copy(total.at[slot], partial.at[slot], out_sem.at[slot])

    @pl.when(polar(lat))
    def _():
        partial_copy(jnp.where(lat == 0, 1, 2)).start()

    def own_share(half, carry):
        squared[...] = jnp.dot(features[2], obs_features[half], preferred_element_type=jnp.float32)
        for lane in range(4):
            lanes = slice(lane * 128, lane * 128 + 128)
            points = [obs_rows[half, c : c + 1, lanes] for c in range(3)]
            weight = [obs_rows[half, 3 + c : 4 + c, lanes] for c in range(3)]
            residual = [tiles[0, half, 3 + c : 4 + c, lanes] for c in range(3)]
            for piece in range(16):
                rows = slice(piece * 16, piece * 16 + 16)
                values = couple(squared[rows, lanes], points, [wide[2, c, rows] for c in range(3)])
                sums = right[rows]
                for c in range(3):
                    value = values[c] * weight[c]
                    weighted[rows, lanes_of(c, lane)] = value.astype(jnp.bfloat16)
                    sums = sums + value * residual[c]
                right[rows] = sums

        def share(turn, inner):
            slot = jnp.where(turn == 0, 0, neighbour(turn - 1))
            product = lax.dot_general(
                weighted[...], low[half, slot], (((1,), (1,)), ((), ())), preferred_element_type=jnp.float32
            )
            total[slot] = total[slot] + product

            @pl.when(half == halves - 1)
            def _():
                partial_copy(slot).start()

            return inner

        return lax.fori_loop(0, jnp.where(polar(lat), 4, 5), share, carry)

    lax.fori_loop(0, halves, own_share, 0)
    rhs[...] = jnp.sum(right[...].T, axis=0, keepdims=True)
    for slot in range(5, len(OFFSETS)):
        dip_arrival(slot)

    for slot in range(1, len(OFFSETS)):

        @pl.when(inside(-OFFSETS[slot][0]))
        def _():
            dip_copy(slot).wait_send()

    for slot in range(1, len(CROSS)):
        step = CROSS[slot][0]

        @pl.when(inside(-step))
        def _():
            obs_copy(slot, 0).wait_recv()

            @pl.when(polar(lat - step))
            def _():
                obs_copy(slot, 1).wait_recv()

        @pl.when(inside(step))
        def _():
            obs_copy(slot, 0).wait_send()

            @pl.when(polar(lat))
            def _():
                obs_copy(slot, 1).wait_send()

    for slot in range(5):
        partial_copy(slot).wait()


def compute(dips, tiles, partial, share, gram, rhs, codes, obs_rows, obs_features, source_features, wide, squared, low_a, low_b, weighted, right, total, slab_s, slab_o, out_sem, in_sem):
    lat = lax.axis_index("lat")
    every = [step_codes(row) for row in range(LAT)]
    passes = by_row(lat, [len(first) for first, rest in every])
    for part, base in ((0, 0), (1, 8)):
        for number in range(max(len(row[part]) for row in every)):
            codes[base + number] = by_row(lat, [row[part][number] if number < len(row[part]) else 0 for row in every])
    partial_copy = pltpu.make_async_copy(partial, total.at[pl.ds(0, 5)], in_sem)
    partial_copy.start()
    centre = dips[0, 4:7, 0:1]

    def source_setup(slot, slab):
        prepare_source(dips[slot], centre, slab, source_features.at[slot], wide.at[slot])

    def obs_setup(slot, carry):
        for half in range(2):
            raw = tiles[slot, half]
            obs_features[slot, half] = point_features(raw, centre, slab_o)
            obs_rows[slot, half, 0:3, :] = raw[0:3, :] * FOLD
            obs_rows[slot, half, 3:6, :] = raw[6:7, :] * HUBER_EDGE / jnp.maximum(jnp.abs(raw[3:6, :]), HUBER_EDGE)
            obs_rows[slot, half, 6:9, :] = raw[3:6, :]
        return carry

    lax.fori_loop(1, 5, obs_setup, 0)
    source_setup(0, slab_s.at[0])
    for slot in range(1, 3):
        source_setup(slot, slab_s.at[slot])

    total[5:] = jnp.zeros_like(total[5:])
    right[...] = jnp.zeros_like(right)

    def square(tile, half, source, to):
        squared[to] = jnp.dot(source_features[source], obs_features[tile, half], preferred_element_type=jnp.float32)

    def add_gram(target, number, low):
        product = lax.dot_general(
            weighted[number], low[...], (((1,), (1,)), ((), ())), preferred_element_type=jnp.float32
        )
        total[target] = total[target] + product

    def own_square(number, to):
        code = codes[number]
        square(code & 15, (code >> 4) & 15, 0, to)

    def own_couple(number, at, low):
        code = codes[number]
        tile, half = code & 15, (code >> 4) & 15
        for lane in range(4):
            lanes = slice(lane * 128, lane * 128 + 128)
            rows_of = [obs_rows[tile, half, c : c + 1, lanes] for c in range(9)]
            for piece in range(16):
                rows = slice(piece * 16, piece * 16 + 16)
                values = couple(squared[at, rows, lanes], rows_of[0:3], [wide[0, c, rows] for c in range(3)])
                sums = right[rows]
                for c in range(3):
                    low[rows, lanes_of(c, lane)] = values[c].astype(jnp.bfloat16)
                    value = values[c] * rows_of[3 + c]
                    weighted[number, rows, lanes_of(c, lane)] = value.astype(jnp.bfloat16)
                    sums = sums + value * rows_of[6 + c]
                right[rows] = sums

    own_square(0, 0)
    buffers = (low_a, low_b)
    fresh = 3
    for number in range(4):
        if number < 3:
            own_square(number + 1, (number + 1) % 2)
        if number == 1:
            partial_copy.wait()
        if number > 0:
            add_gram(0, number - 1, buffers[(number - 1) % 2])
        for piece in range(3 if number < 2 else 2):
            source_setup(fresh, slab_s.at[piece])
            fresh += 1
        own_couple(number, number % 2, buffers[number % 2])
    add_gram(0, 3, buffers[1])

    def more_own(number, carry):
        own_square(number, 0)
        own_couple(number, 0, low_a)
        add_gram(0, number, low_a)
        return carry

    lax.fori_loop(4, passes, more_own, 0)

    def decode(step):
        code = codes[8 + step]
        return code & 15, (code >> 4) & 15, (code >> 8) & 15, (code >> 12) & 15, code >> 16

    def square_step(step, to):
        tile, half, number, source, target = decode(step)
        square(tile, half, source, to)

    def couple_step(step, at, low):
        tile, half, number, source, target = decode(step)
        for lane in range(4):
            lanes = slice(lane * 128, lane * 128 + 128)
            points = [obs_rows[tile, half, c : c + 1, lanes] for c in range(3)]
            for piece in range(16):
                rows = slice(piece * 16, piece * 16 + 16)
                values = couple(squared[at, rows, lanes], points, [wide[source, c, rows] for c in range(3)])
                for c in range(3):
                    low[rows, lanes_of(c, lane)] = values[c].astype(jnp.bfloat16)

    def gram_step(step, low):
        tile, half, number, source, target = decode(step)
        add_gram(target, number, low)

    square_step(0, 0)
    square_step(1, 1)
    couple_step(0, 0, low_a)

    def steps_from(start, count):
        for ahead in range(count):
            step = start + ahead
            before, after = (low_a, low_b) if ahead % 2 == 0 else (low_b, low_a)
            square_step(step + 2, ahead % 2)
            gram_step(step, before)
            couple_step(step + 1, (ahead + 1) % 2, after)

    def some_steps(group, carry):
        steps_from(UNROLL * group, UNROLL)
        return carry

    lax.fori_loop(0, (STEPS - 2) // UNROLL, some_steps, 0)
    def out_copy(first, count, at):
        blocks = pl.ds(first, count)
        return pltpu.make_async_copy(total.at[blocks], gram.at[blocks], out_sem.at[at])

    early = [out_copy(0, 3, 0), out_copy(4, 3, 1), out_copy(8, 5, 2)]
    late = [out_copy(block, 1, 3 + at) for at, block in enumerate(LAST)]
    for copy in early:
        copy.start()
    gram_step(STEPS - 2, low_a)
    late[0].start()
    couple_step(STEPS - 1, 1, low_b)
    gram_step(STEPS - 1, low_b)
    late[1].start()
    rhs[...] = share[...] + jnp.sum(right[...].T, axis=0, keepdims=True)
    for copy in early + late:
        copy.wait()


def shards(obs_frac, obs_field, dipole_frac, dipole_moment, obs_count):
    vmem = pl.BlockSpec(memory_space=pltpu.VMEM)
    slots = len(OFFSETS) + 1
    f32, low = jnp.float32, jnp.bfloat16
    dips, tiles, partial, share = pl.pallas_call(
        exchange,
        out_shape=(
            jax.ShapeDtypeStruct((slots, 8, BS), f32),
            jax.ShapeDtypeStruct((5, 2, 8, HALF), f32),
            jax.ShapeDtypeStruct((5, BS, BS), f32),
            jax.ShapeDtypeStruct((1, BS), f32),
        ),
        in_specs=[pl.BlockSpec(memory_space=pltpu.SMEM)] + [pl.BlockSpec(memory_space=pl.ANY)] * 4,
        out_specs=(vmem, vmem, pl.BlockSpec(memory_space=pl.ANY), vmem),
        scratch_shapes=[
            pltpu.VMEM((2, 8, HALF), f32),
            pltpu.VMEM((2, FEATURES, HALF), low),
            pltpu.VMEM((3, BS, FEATURES), low),
            pltpu.VMEM((3, 4, BS, 128), f32),
            pltpu.VMEM((BS, HALF), f32),
            pltpu.VMEM((2, 16, 3 * HALF), f32),
            pltpu.VMEM((2, 5, BS, 3 * HALF), low),
            pltpu.VMEM((BS, 3 * HALF), low),
            pltpu.VMEM((BS, 128), f32),
            pltpu.VMEM((5, BS, BS), f32),
            pltpu.VMEM((FEATURES, BS), f32),
            pltpu.VMEM((FEATURES, HALF), f32),
            pltpu.SemaphoreType.DMA((len(OFFSETS),)),
            pltpu.SemaphoreType.DMA((len(OFFSETS),)),
            pltpu.SemaphoreType.DMA((len(CROSS), 2)),
            pltpu.SemaphoreType.DMA((len(CROSS), 2)),
            pltpu.SemaphoreType.DMA((5,)),
            pltpu.VMEM((2, OBS), f32),
            pltpu.VMEM((3, 1, OBS), f32),
            pltpu.VMEM((2, BS), f32),
            pltpu.VMEM((1, BS), f32),
            pltpu.SemaphoreType.DMA((4,)),
        ],
        compiler_params=pltpu.CompilerParams(
            collective_id=0, has_side_effects=True, vmem_limit_bytes=60 * 2**20
        ),
        name="exchange",
    )(obs_count, obs_frac[0, 0], jnp.transpose(obs_field[0], (1, 0, 2)), dipole_frac[0, 0], dipole_moment[0])
    gram, rhs = compute_call(dips, tiles, partial, share)
    return gram[None, None], rhs[None]


def compute_call(dips, tiles, partial, share):
    vmem = pl.BlockSpec(memory_space=pltpu.VMEM)
    slots = len(OFFSETS) + 1
    f32, low = jnp.float32, jnp.bfloat16
    return pl.pallas_call(
        compute,
        out_shape=(jax.ShapeDtypeStruct((13, BS, BS), f32), jax.ShapeDtypeStruct((1, BS), f32)),
        in_specs=[vmem, vmem, pl.BlockSpec(memory_space=pl.ANY), vmem],
        out_specs=(pl.BlockSpec(memory_space=pl.ANY), vmem),
        scratch_shapes=[
            pltpu.SMEM((32,), jnp.int32),
            pltpu.VMEM((5, 2, 16, HALF), f32),
            pltpu.VMEM((5, 2, FEATURES, HALF), low),
            pltpu.VMEM((slots, BS, FEATURES), low),
            pltpu.VMEM((slots, 3, BS, 128), f32),
            pltpu.VMEM((2, BS, HALF), f32),
            pltpu.VMEM((BS, 3 * HALF), low),
            pltpu.VMEM((BS, 3 * HALF), low),
            pltpu.VMEM((5, BS, 3 * HALF), low),
            pltpu.VMEM((BS, 128), f32),
            pltpu.VMEM((slots, BS, BS), f32),
            pltpu.VMEM((3, FEATURES, BS), f32),
            pltpu.VMEM((FEATURES, HALF), f32),
            pltpu.SemaphoreType.DMA((5,)),
            pltpu.SemaphoreType.DMA,
        ],
        compiler_params=pltpu.CompilerParams(vmem_limit_bytes=60 * 2**20),
        name="normal_blocks",
    )(dips, tiles, partial, share)


def solution(mesh):
    in_specs = (
        P("lat", "lon", None, None),
        P("lat", "lon", None, None),
        P("lat", "lon", None, None),
        P("lat", "lon", None),
        P("lat", "lon"),
    )
    out_specs = (P("lat", "lon", None, None, None), P("lat", "lon", None))
    return jax.shard_map(shards, mesh=mesh, in_specs=in_specs, out_specs=out_specs, check_vma=False)
```
